128 devices in a mesh: dp: 16 (over y, z_hi, core), mp: 8 (over z_lo, x).
Axes of the slice: x: 4, y: 4, z: 4 (z_hi: 2, z_lo: 2; z = z_hi * 2 + z_lo), core: 2. Of those that a mesh axis runs over, the one named last changes fastest.
Arguments:
- patches: bfloat16 [2048, 6144], P('dp'), may hold values from -6 to 6
- patch_pos: int32 [2048], P('dp'), may hold values from 0 to 1023
- tile_counts: int32 [8], P('mp'), may hold values from 1 to 4, as said below
- pos_table: bfloat16 [1024, 6144], replicated, may hold values from -3 to 3
- w_qkv: bfloat16 [6144, 3, 4096], P('mp', None, 'dp'), may hold values from -0.078125 to 0.078125
- qk_gain: float32 [2, 128], replicated, may hold values from 0.5 to 9
- w_attn_out: bfloat16 [4096, 6144], P('dp', 'mp'), may hold values from -0.09375 to 0.09375
- w_mlp_in: bfloat16 [6144, 12288], P('mp', 'dp'), may hold values from -0.078125 to 0.078125
- mlp_bias: float32 [12288], P('dp'), may hold values from -3 to 3
- w_mlp_out: bfloat16 [12288, 6144], P('dp', 'mp'), may hold values from -0.0546875 to 0.0546875
- norm_gain: float32 [6144], replicated, may hold values from 0.25 to 1.75
Outputs:
- encoded: bfloat16 [2048, 6144], P(('dp', 'mp'))
The draws below stay inside these ranges and needn't reach their ends.
Inputs may be any that keep to these rules, and one draw needn't show every extreme that they name: `tile_counts`: every draw has an image with 4 tiles.
All inputs are finite; a program needn't handle non-finite values.
Results may differ from the reference program's by a relative error of at most 0.03.
Values may be sent and summed in bfloat16 or wider, within the bound.
No kernel may reach another device: no remote copies, remote signals or barrier semaphores. Data moves between devices by JAX's collectives and lax.ppermute only.
A program may use at most 128 MiB of HBM per device.

```python
import jax
import jax.numpy as jnp
from jax import lax

D = 6144
HS = 128
HEADS = 32
FF = 12288
PATCHES = 256
TILE = 64
GRID = 1024
TOKENS = 2048
IMAGES = 8
TILES = 4


def draw_tile_counts(key, part):
    key = jax.random.fold_in(key, 11)
    counts = jax.random.randint(key, (IMAGES,), 1, TILES + 1)
    counts = counts.at[0].set(TILES)
    return counts.astype(jnp.int32)


def draw_qk_gain(key, part):
    key = jax.random.fold_in(key, 23)
    gains = jnp.exp(jax.random.uniform(key, (2, HS), jnp.float32, -0.69, 0.69))
    return gains.astype(jnp.float32)


def touch_ends(result, own_key, smallest, high):
    place = [jax.random.randint(jax.random.fold_in(own_key, axis), (), 0, length) for axis, length in enumerate(result.shape)]
    longest = result.shape.index(max(result.shape))
    neighbour = place[:longest] + [(place[longest] + 1) % result.shape[longest]] + place[longest + 1:]
    return result.at[tuple(place)].set(smallest).at[tuple(neighbour)].set(high)


def steps_of(rng, extent, cuts, low, largest):
    def one(position, blocks):
        heights = jax.random.uniform(jax.random.fold_in(jax.random.fold_in(rng, 6), position), (blocks,), jnp.float32, low / len(cuts), largest / len(cuts))
        return jnp.repeat(jnp.exp(heights), extent[position] // blocks).reshape((-1,) + (1,) * (len(extent) - position - 1))

    factor_of = one(*cuts[0])
    for cut in cuts[1:]:
        factor_of = factor_of * one(*cut)
    return factor_of


def bell_draw(stream_key, extent, deviation, bound, cuts=(), kind=jnp.bfloat16):
    loudness = steps_of(stream_key, extent, cuts, -0.22, 0.18) if cuts else 1.0
    values = jax.random.normal(stream_key, extent, jnp.float32) * deviation * loudness
    return jnp.minimum(jnp.maximum(values, -bound), bound).astype(kind)


def setup_inputs(seed: int = 0) -> dict:
    splits = jax.random.split(jax.random.key(seed), 12)
    return {
        "patches": bell_draw(splits[0], (TOKENS, D), 1.0, 6.0, ((0, 16),)),
        "patch_pos": touch_ends(jax.random.randint(splits[1], (TOKENS,), 0, GRID), jax.random.fold_in(splits[1], 1), 0, GRID - 1).astype(jnp.int32),
        "tile_counts": draw_tile_counts(jax.random.fold_in(splits[11], 71), 0),
        "pos_table": bell_draw(splits[3], (GRID, D), 0.5, 3.0),
        "w_qkv": bell_draw(splits[4], (D, 3, HEADS * HS), D ** -0.5, 0.078125, ((0, 8), (2, 16))),
        "qk_gain": draw_qk_gain(jax.random.fold_in(splits[11], 71), 0),
        "w_attn_out": bell_draw(splits[6], (HEADS * HS, D), (HEADS * HS) ** -0.5, 0.09375, ((0, 16), (1, 8))),
        "w_mlp_in": bell_draw(splits[7], (D, FF), D ** -0.5, 0.078125, ((0, 8), (1, 16))),
        "mlp_bias": bell_draw(splits[8], (FF,), 0.5, 3.0, ((0, 16),), jnp.float32),
        "w_mlp_out": bell_draw(splits[9], (FF, D), FF ** -0.5, 0.0546875, ((0, 16), (1, 8))),
        "norm_gain": jnp.clip(1.0 + 0.15 * jax.random.normal(splits[10], (D,), jnp.float32), 0.25, 1.75),
    }


norm_eps = 1e-06

def layer_norm(vector, gain_vec):
    average = lax.optimization_barrier(jnp.mean(vector, axis=-1, keepdims=True))
    centered = vector - average
    variance = lax.optimization_barrier(jnp.mean(centered * centered, axis=-1, keepdims=True))
    return centered * lax.rsqrt(variance + norm_eps) * gain_vec

def reference(patches, patch_pos, tile_counts, pos_table, w_qkv, qk_gain, w_attn_out, w_mlp_in, mlp_bias, w_mlp_out, norm_gain):
    embedded = patches.astype(jnp.float32) + pos_table.astype(jnp.float32)[patch_pos]
    residual = embedded.astype(jnp.bfloat16)
    normed = layer_norm(residual.astype(jnp.float32), norm_gain).astype(jnp.bfloat16)
    head_cols = HEADS * HS
    qkv = jnp.dot(normed, w_qkv.reshape(D, 3 * head_cols), preferred_element_type=jnp.float32)
    preact = jnp.dot(normed, w_mlp_in, preferred_element_type=jnp.float32)
    shape4 = (IMAGES, PATCHES, HEADS, HS)
    queries = layer_norm(qkv[:, :head_cols].reshape(TOKENS, HEADS, HS), qk_gain[0]).astype(jnp.bfloat16).reshape(shape4)
    key_rows = layer_norm(qkv[:, head_cols:2 * head_cols].reshape(TOKENS, HEADS, HS), qk_gain[1]).astype(jnp.bfloat16).reshape(shape4)
    value_rows = qkv[:, 2 * head_cols:].astype(jnp.bfloat16).reshape(shape4)
    scores = jnp.einsum('iqhd,ikhd->ihqk', queries.astype(jnp.float32), key_rows.astype(jnp.float32)) * HS ** (-0.5)
    slots = jnp.arange(PATCHES, dtype=jnp.int32)
    live = slots[None, :] < (tile_counts * TILE)[:, None]
    scores = jnp.where(live[:, None, None, :], scores, -1e+30)
    row_max = lax.optimization_barrier(jnp.max(scores, axis=-1, keepdims=True))
    lifted = jnp.exp(scores - row_max)
    probs = (lifted / lax.optimization_barrier(jnp.sum(lifted, axis=-1, keepdims=True))).astype(jnp.bfloat16)
    attended = jnp.einsum('ihqk,ikhd->iqhd', probs.astype(jnp.float32), value_rows.astype(jnp.float32))
    attended = attended.reshape(TOKENS, head_cols).astype(jnp.bfloat16)
    hidden = jax.nn.gelu(preact + mlp_bias, approximate=False).astype(jnp.bfloat16)
    attn_term = jnp.dot(attended, w_attn_out, preferred_element_type=jnp.float32)
    mlp_term = jnp.dot(hidden, w_mlp_out, preferred_element_type=jnp.float32)
    return (residual.astype(jnp.float32) + attn_term + mlp_term).astype(jnp.bfloat16)
```

```python
import itertools

import jax
import jax.numpy as jnp
from jax import lax
from jax.sharding import Mesh, PartitionSpec as P

PATCHES = 256
TILE = 64
AXES = ("y", "zh", "c", "zl", "x")
SIZES = {"y": 4, "zh": 2, "c": 2, "zl": 2, "x": 4}
bf16 = jnp.bfloat16
f32 = jnp.float32
norm_eps = 1e-06


def pairs(place):
    out = []
    for spot in itertools.product(*[range(SIZES[a]) for a in AXES]):
        here = dict(zip(AXES, spot))
        there = place(dict(here))
        ends = []
        for point in (here, there):
            index = 0
            for a in AXES:
                index = index * SIZES[a] + point[a] % SIZES[a]
            ends.append(index)
        out.append(tuple(ends))
    return out


def send(value, **shift):
    def place(d):
        for a, by in shift.items():
            d[a] += by
        return d

    return lax.ppermute(value, AXES, pairs(place))


def cross(value, by=0):
    def place(d):
        d["zh"], d["zl"] = d["zl"], d["zh"]
        d["x"] += by
        return d

    return lax.ppermute(value, AXES, pairs(place))


def head_norm(vector, gain_vec):
    average = jnp.mean(vector, axis=-1, keepdims=True)
    centered = vector - average
    variance = jnp.mean(centered * centered, axis=-1, keepdims=True)
    return centered * lax.rsqrt(variance + norm_eps) * gain_vec


def dot(a, b):
    return jnp.dot(a, b, preferred_element_type=f32)


def pick(blocks, index):
    return lax.dynamic_index_in_dim(blocks, index, 0, keepdims=False)


def shards(
    patches,
    patch_pos,
    tile_counts,
    pos_table,
    w_qkv,
    qk_gain,
    w_attn_out,
    w_mlp_in,
    mlp_bias,
    w_mlp_out,
    norm_gain,
):
    y, zh, c, zl, x = [lax.axis_index(a) for a in AXES]
    width = patches.shape[1]
    cols = w_mlp_in.shape[0]
    rows = patches.shape[0]
    starts = [(zl * 4 + x) * cols, ((1 - zl) * 4 + x) * cols]

    wq = jnp.transpose(w_qkv, (1, 0, 2))
    heads = w_qkv.shape[2] // 128

    def gather_weight(w):
        other = send(w, zl=1)
        return [[w, other], [send(w, c=1), send(other, c=1)]]

    onehot = (patch_pos[:, None] == jnp.arange(pos_table.shape[0], dtype=jnp.int32)[None, :]).astype(bf16)
    own = []
    for s in starts:
        e = lax.dynamic_slice_in_dim(patches, s, cols, 1).astype(f32) + dot(
            onehot, lax.dynamic_slice_in_dim(pos_table, s, cols, 1)
        )
        own.append(e.astype(bf16))
    own = jnp.stack(own)
    away = cross(own)
    own = jnp.where(zh == zl, own, away[::-1])
    parts = jnp.stack([own] + [send(own, y=k) for k in (1, 2, 3)])
    gains = jnp.stack([lax.dynamic_slice_in_dim(norm_gain, s, cols, 0) for s in starts])
    parts_f = parts.astype(f32)
    mean = jnp.mean(parts_f, axis=(1, 3))
    m2 = jnp.sum((parts_f - mean[:, None, :, None]) ** 2, axis=(1, 3))
    stats = jnp.stack([mean, m2])
    all_stats = jnp.stack([stats] + [send(stats, x=k) for k in (1, 2, 3)])
    mu = jnp.mean(all_stats[:, 0], axis=0)
    var = (
        jnp.sum(all_stats[:, 1], axis=0)
        + 2 * cols * jnp.sum((all_stats[:, 0] - mu[None]) ** 2, axis=0)
    ) / width
    scale = lax.rsqrt(var + norm_eps)
    normed = ((parts_f - mu[:, None, :, None]) * scale[:, None, :, None] * gains[None, :, None, :]).astype(bf16)

    wqs = gather_weight(wq)
    wms = gather_weight(w_mlp_in)
    outs = [gather_weight(w_attn_out), gather_weight(w_mlp_out)]

    blocks = [pick(normed, (y - x - k) % 4) for k in range(4)]

    def project(ws):
        res = []
        for k in range(4):
            b = blocks[k]
            p = jnp.concatenate([dot(b[0], w[0]) + dot(b[1], w[1]) for w in ws], axis=1)
            res.append(p)
        total = res[0]
        for k in (2, 1, 3):
            total = total + send(res[k].astype(bf16), x=k).astype(f32)
        return total

    qkv_ws = [[w[0][i], w[1][i]] for i in range(3) for w in wqs]
    qkv = project(qkv_ws)
    qkv = qkv.reshape(rows, 3, 2, heads, 128)
    queries = head_norm(qkv[:, 0], qk_gain[0]).astype(bf16)
    keys = head_norm(qkv[:, 1], qk_gain[1]).astype(bf16)
    vals = qkv[:, 2].astype(bf16)
    kv = jnp.stack([keys, vals])
    kv_far = send(kv[:, :, ::-1], c=1)
    counts = lax.ppermute(
        tile_counts,
        AXES,
        pairs(lambda d: dict(d, x=(d["zl"] * 4 + d["x"]) // 2, zl=(d["zl"] * 4 + d["x"]) % 2)),
    )
    slots = jnp.arange(rows, dtype=jnp.int32)
    slots = jnp.concatenate([c * rows + slots, (1 - c) * rows + slots])
    live = slots < counts[0] * TILE
    kv = jnp.concatenate([kv, kv_far], axis=1)
    scores = jnp.einsum("qghd,kghd->ghqk", queries, kv[0], preferred_element_type=f32) * 128 ** (-0.5)
    scores = jnp.where(live, scores, -1e30)
    lifted = jnp.exp(scores - jnp.max(scores, axis=-1, keepdims=True))
    probs = (lifted / jnp.sum(lifted, axis=-1, keepdims=True)).astype(bf16)
    attended = jnp.einsum("ghqk,kghd->qghd", probs, kv[1], preferred_element_type=f32)
    attended = attended.reshape(rows, -1).astype(bf16)

    bias = jnp.concatenate([mlp_bias, send(mlp_bias, c=1)])
    pre = project(wms) + bias
    hidden = jax.nn.gelu(pre, approximate=False).astype(bf16)

    att_all = jnp.stack([attended] + [send(attended, x=k) for k in (1, 2, 3)])
    hid_all = jnp.stack([hidden] + [send(hidden, x=k) for k in (1, 2, 3)])
    acols = attended.shape[1] // 2
    hcols = hidden.shape[1] // 2
    total = None
    half = rows // 2
    ab = []
    for j in range(4):
        k = (x - y - j) % 4
        a, h = pick(att_all, k), pick(hid_all, k)
        out = []
        for side in range(2):
            o = None
            for core in range(2):
                t = dot(a[:, core * acols : (core + 1) * acols], outs[0][core][side])
                t = t + dot(h[:, core * hcols : (core + 1) * hcols], outs[1][core][side])
                o = t if o is None else o + t
            out.append(o)
        ab.append(jnp.concatenate(out, axis=1))
    for j in (0, 2, 1, 3):
        near = lax.dynamic_slice_in_dim(ab[j], zh * half, half, 0)
        far = lax.dynamic_slice_in_dim(ab[j], (1 - zh) * half, half, 0)
        if j == 0:
            total = near
        else:
            total = total + send(near.astype(bf16), y=j).astype(f32)
        total = total + send(far.astype(bf16), y=j, zh=1).astype(f32)
    res = lax.dynamic_slice_in_dim(own, zh * half, half, 1)
    res = jnp.concatenate([res[0], res[1]], axis=1).astype(f32)
    done = (total + res).astype(bf16)
    final = jnp.zeros((half // 4, 8, cols), bf16)
    for k in range(4):
        piece = lax.dynamic_slice_in_dim(done, ((x + k) % 4) * (half // 4), half // 4, 0)
        got = cross(piece, k).reshape(half // 4, 2, cols)
        at = (x - k) % 4
        final = lax.dynamic_update_slice_in_dim(final, got[:, 0:1], zh * 4 + at, 1)
        final = lax.dynamic_update_slice_in_dim(final, got[:, 1:2], (1 - zh) * 4 + at, 1)
    return final.reshape(half // 4, width)


def solution(mesh):
    fine = Mesh(mesh.devices.reshape([SIZES[a] for a in AXES]), AXES)
    dp, mp = ("y", "zh", "c"), ("zl", "x")
    placed = (
        P(dp, None),
        P(dp),
        P(mp),
        P(),
        P(mp, None, dp),
        P(),
        P(dp, mp),
        P(mp, dp),
        P(dp),
        P(dp, mp),
        P(),
    )
    return jax.shard_map(shards, mesh=fine, in_specs=placed, out_specs=P(dp + mp, None), check_vma=False)
```

```python
import functools
import itertools

import jax
import jax.numpy as jnp
from jax import lax
from jax.experimental import pallas as pl
from jax.experimental.pallas import tpu as pltpu
from jax.sharding import Mesh, PartitionSpec as P

TILE = 64
HS = 128
AXES = ("y", "zh", "c", "zl", "x")
SIZES = {"y": 4, "zh": 2, "c": 2, "zl": 2, "x": 4}
bf16 = jnp.bfloat16
f32 = jnp.float32
norm_eps = 1e-06


def limit(mib):
    return pltpu.CompilerParams(vmem_limit_bytes=mib * 2**20)


CHEAP = pl.CostEstimate(flops=1000, bytes_accessed=1000, transcendentals=0)


def pairs(place):
    out = []
    for spot in itertools.product(*[range(SIZES[a]) for a in AXES]):
        here = dict(zip(AXES, spot))
        there = place(dict(here))
        ends = []
        for point in (here, there):
            index = 0
            for a in AXES:
                index = index * SIZES[a] + point[a] % SIZES[a]
            ends.append(index)
        out.append(tuple(ends))
    return out


def route(value, place):
    return lax.ppermute(value, AXES, pairs(place))


def send(value, **shift):
    def place(d):
        for a, by in shift.items():
            d[a] += by
        return d

    return route(value, place)


def cross(value, by=0):
    def place(d):
        d["zh"], d["zl"] = d["zl"], d["zh"]
        d["x"] += by
        return d

    return route(value, place)


def after(value, *others):
    return lax.optimization_barrier((value, *others))[0]


def dot(a, b):
    return jnp.dot(a, b, preferred_element_type=f32)


def whole(shape):
    return pl.BlockSpec(shape, lambda *_: (0,) * len(shape))


def shape_of(*shape, dtype=bf16):
    return jax.ShapeDtypeStruct(shape, dtype)


def lookup(chosen, refs):
    few = refs[0].shape[0]
    parts = [dot(chosen[:, i * few : (i + 1) * few], ref[...]) for i, ref in enumerate(refs)]
    return parts[0] + parts[1] + parts[2] + parts[3]


def choose(pos_ref, chosen):
    rows, slots = chosen.shape
    at = jnp.broadcast_to(pos_ref[...].astype(f32), (rows, rows)).T[:, 0:1]
    spots = lax.broadcasted_iota(jnp.int32, (rows, slots), 1)
    chosen[...] = (spots == at.astype(jnp.int32)).astype(f32).astype(bf16)


def measure_kernel(patches_ref, pos_ref, t0, t1, t2, t3, out_ref, chosen, means, devs):
    j, blocks = pl.program_id(0), pl.num_programs(0)
    rows, cols = patches_ref.shape

    @pl.when(j == 0)
    def _():
        choose(pos_ref, chosen)
        means[...] = jnp.zeros_like(means)
        devs[...] = jnp.zeros_like(devs)

    e = (patches_ref[...].astype(f32) + lookup(chosen, (t0, t1, t2, t3))).astype(bf16).astype(f32)
    mean = jnp.mean(e, axis=1, keepdims=True)
    dev = jnp.sum((e - mean) ** 2, axis=1, keepdims=True)
    lane = lax.broadcasted_iota(jnp.int32, (rows, 128), 1)
    means[...] = jnp.where(lane == j, mean, means[...])
    devs[...] = jnp.where(lane == j, dev, devs[...])

    @pl.when(j == blocks - 1)
    def _():
        count = blocks
        mu = jnp.sum(means[...], axis=1, keepdims=True) / count
        apart = jnp.where(lane < blocks, (means[...] - mu) ** 2, 0.0)
        total = jnp.sum(devs[...], axis=1, keepdims=True) + cols * jnp.sum(apart, axis=1, keepdims=True)
        scale = lax.rsqrt(total / (cols * count) + norm_eps)
        out_ref[...] = jnp.where(lane == 0, mu, scale).T[:8]


def measure(patches, pos, table, blocks):
    rows, cols, few = patches.shape[0], patches.shape[1] // blocks, table.shape[0] // 4
    return pl.pallas_call(
        measure_kernel,
        grid=(blocks,),
        in_specs=[pl.BlockSpec((rows, cols), lambda j: (0, j)), whole((1, rows))]
        + [pl.BlockSpec((few, cols), functools.partial(lambda i, j: (i, j), i)) for i in range(4)],
        out_specs=whole((8, rows)),
        out_shape=shape_of(8, rows, dtype=f32),
        scratch_shapes=[
            pltpu.VMEM((rows, table.shape[0]), bf16),
            pltpu.VMEM((rows, 128), f32),
            pltpu.VMEM((rows, 128), f32),
        ],
        compiler_params=limit(52),
        cost_estimate=CHEAP,
        name="measure",
    )(patches, pos, table, table, table, table)


def embed_kernel(info_ref, patches_ref, pos_ref, stat_ref, gain_ref, t0, t1, t2, t3, e_ref, normed_ref, chosen):
    @pl.when(pl.program_id(0) == 0)
    def _():
        choose(pos_ref, chosen)

    e = (patches_ref[0].astype(f32) + lookup(chosen, (t0, t1, t2, t3))).astype(bf16)
    e_ref[0] = e
    rows = e.shape[0]
    turned = jnp.concatenate([stat_ref[...]] * (rows // 8), axis=0).T
    normed_ref[0] = ((e.astype(f32) - turned[:, 0:1]) * turned[:, 1:2] * gain_ref[...]).astype(bf16)


def embed(info, patches, pos, stat, table, gain):
    _, rows, cols = patches.shape
    few = table.shape[0] // 4
    return pl.pallas_call(
        embed_kernel,
        grid_spec=pltpu.PrefetchScalarGridSpec(
            num_scalar_prefetch=1,
            grid=(2,),
            in_specs=[
                pl.BlockSpec((1, rows, cols), lambda s, info: (s, 0, 0)),
                pl.BlockSpec((1, rows), lambda s, info: (0, 0)),
                pl.BlockSpec((8, rows), lambda s, info: (0, 0)),
                pl.BlockSpec((1, cols), lambda s, info: (0, info[2 + s])),
            ]
            + [pl.BlockSpec((few, cols), functools.partial(lambda i, s, info: (i, info[2 + s]), i)) for i in range(4)],
            out_specs=[pl.BlockSpec((1, rows, cols), lambda s, info: (s, 0, 0))] * 2,
            scratch_shapes=[pltpu.VMEM((rows, table.shape[0]), bf16)],
        ),
        out_shape=[shape_of(2, rows, cols)] * 2,
        compiler_params=limit(52),
        cost_estimate=CHEAP,
        name="embed",
    )(info, patches, pos, stat, gain, table, table, table, table)


def project_kernel(info_ref, x0, x1, x2, x3, w00, w01, w10, w11, o0, o1, o2, o3, held):
    rows = x0.shape[1]
    zl, x = info_ref[1], info_ref[2]

    @pl.when(pl.program_id(0) == 0)
    def _():
        for far, ref in enumerate((x0, x1, x2, x3)):
            k = lax.rem(8 - x - far, 4)
            for s in range(2):
                held[s, pl.ds(pl.multiple_of(k * rows, rows), rows)] = ref[lax.rem(zl + s, 2)]

    def weight(ref):
        w = ref[...]
        return w.reshape(w.shape[-2:])

    for core, (near, far) in enumerate(((w00, w01), (w10, w11))):
        got = dot(held[0], weight(near)) + dot(held[1], weight(far))
        n = got.shape[1]
        for k, ref in enumerate((o0, o1, o2, o3)):
            ref[:, core * n : (core + 1) * n] = got[k * rows : (k + 1) * rows].astype(ref.dtype)


def project(info, xs, ws):
    _, rows, depth = xs[0].shape
    if ws[0].ndim == 3:
        spec = pl.BlockSpec((1, depth, ws[0].shape[2]), lambda i: (i, 0, 0))
        steps, n = ws[0].shape[0], 2 * ws[0].shape[2]
    else:
        n = 512
        spec = pl.BlockSpec((depth, n // 2), lambda i: (0, i))
        steps = 2 * ws[0].shape[1] // n
    return pl.pallas_call(
        project_kernel,
        grid=(steps,),
        in_specs=[pl.BlockSpec(memory_space=pltpu.SMEM)] + [whole((2, rows, depth))] * 4 + [spec] * 4,
        out_specs=[pl.BlockSpec((rows, n), lambda i: (0, i))] * 4,
        out_shape=[shape_of(rows, steps * n, dtype=f32 if k == 0 else bf16) for k in range(4)],
        scratch_shapes=[pltpu.VMEM((2, 4 * rows, depth), bf16)],
        compiler_params=limit(20),
        cost_estimate=CHEAP,
        name="project",
    )(info, *xs, *ws)


def heads_kernel(p0, p1, p2, p3, gain_ref, q_ref, kv_ref):
    part = pl.program_id(0)
    gain = gain_ref[pl.ds(jnp.minimum(part, 1), 1)]
    for h in range(q_ref.shape[1] // HS):
        at = slice(h * HS, (h + 1) * HS)
        v = p0[:, at] + p1[:, at].astype(f32) + p2[:, at].astype(f32) + p3[:, at].astype(f32)
        centered = v - jnp.mean(v, axis=1, keepdims=True)
        spread = lax.rsqrt(jnp.mean(centered * centered, axis=1, keepdims=True) + norm_eps)
        normed = (centered * spread * gain).astype(bf16)

        @pl.when(part == 0)
        def _():
            q_ref[:, at] = normed

        @pl.when(part > 0)
        def _():
            kv_ref[0, :, at] = jnp.where(part == 1, normed.astype(f32), v).astype(bf16)


def head_values(parts, gain):
    rows, n = parts[0].shape[0], parts[0].shape[1] // 3
    return pl.pallas_call(
        heads_kernel,
        grid=(3,),
        in_specs=[pl.BlockSpec((rows, n), lambda i: (0, i))] * 4 + [whole(gain.shape)],
        out_specs=[whole((rows, n)), pl.BlockSpec((1, rows, n), lambda i: (jnp.maximum(i - 1, 0), 0, 0))],
        out_shape=[shape_of(rows, n), shape_of(2, rows, n)],
        compiler_params=limit(8),
        cost_estimate=CHEAP,
        name="heads",
    )(*parts, gain)


def hidden_kernel(att_ref, p0, p1, p2, p3, b0, b1, out_ref):
    step = pl.program_id(0)

    @pl.when(step == 0)
    def _():
        out_ref[...] = att_ref[...]

    @pl.when(step > 0)
    def _():
        bias = jnp.concatenate([b0[...], b1[...]], axis=1)
        v = p0[...] + p1[...].astype(f32) + p2[...].astype(f32) + p3[...].astype(f32) + bias
        out_ref[...] = (v * 0.5 * (1.0 + lax.erf(v * 0.5**0.5))).astype(bf16)


def hidden_units(attended, parts, bias, bias_far):
    rows, n = attended.shape
    steps = parts[0].shape[1] // n

    def block(i):
        return 0, jnp.maximum(i - 1, 0)

    return pl.pallas_call(
        hidden_kernel,
        grid=(1 + steps,),
        in_specs=[whole((rows, n))] + [pl.BlockSpec((rows, n), block)] * 4 + [pl.BlockSpec((1, n // 2), block)] * 2,
        out_specs=pl.BlockSpec((rows, n), lambda i: (0, i)),
        out_shape=shape_of(rows, (1 + steps) * n),
        compiler_params=limit(8),
        cost_estimate=CHEAP,
        name="hidden",
    )(attended, *parts, bias, bias_far)


def attend_kernel(info_ref, count_ref, q_ref, near_ref, far_ref, out_ref):
    core, live = info_ref[4], count_ref[0] * TILE
    rows, n = q_ref.shape
    slot = lax.broadcasted_iota(jnp.int32, (rows, rows), 1)
    heads = n // HS
    for h in range(heads):
        at = slice(h * HS, (h + 1) * HS)
        o = (h + heads // 2) % heads
        other = slice(o * HS, (o + 1) * HS)
        q = q_ref[:, at]
        score = []
        for k, first in ((near_ref[0, :, at], core * rows), (far_ref[0, :, other], (1 - core) * rows)):
            s = lax.dot_general(q, k, (((1,), (1,)), ((), ())), preferred_element_type=f32) * HS ** (-0.5)
            score.append(jnp.where(slot + first < live, s, -1e30))
        top = jnp.maximum(jnp.max(score[0], axis=1, keepdims=True), jnp.max(score[1], axis=1, keepdims=True))
        lifted = [jnp.exp(s - top) for s in score]
        total = jnp.sum(lifted[0], axis=1, keepdims=True) + jnp.sum(lifted[1], axis=1, keepdims=True)
        probs = [(v / total).astype(bf16) for v in lifted]
        out_ref[:, at] = (dot(probs[0], near_ref[1, :, at]) + dot(probs[1], far_ref[1, :, other])).astype(bf16)


def attend(info, count, q, near, far):
    return pl.pallas_call(
        attend_kernel,
        in_specs=[pl.BlockSpec(memory_space=pltpu.SMEM)] * 2 + [pl.BlockSpec(memory_space=pltpu.VMEM)] * 3,
        out_shape=shape_of(*q.shape),
        compiler_params=limit(6),
        cost_estimate=CHEAP,
        name="attend",
    )(info, count, q, near, far)


def output_kernel(info_ref, e_ref, *refs):
    u_refs, weights, outs = refs[0:4], refs[4:8], refs[8:16]
    held, total = refs[16], refs[17]
    step = pl.program_id(0)
    rows, a_cols = u_refs[0].shape[0], u_refs[0].shape[1] // 4
    half, n = rows // 2, total.shape[1]
    zh, zl, x = info_ref[0], info_ref[1], info_ref[2]

    @pl.when(step == 0)
    def _():
        for k in range(4):
            held[k * rows : (k + 1) * rows] = u_refs[k][...]

    def multiply(ws, side):
        depth = a_cols // 2
        few = (ws[0].shape[0] - depth) // 3
        acc = None
        for core in range(2):
            t = dot(held[:, core * depth : (core + 1) * depth], ws[core][:depth])
            acc = t if acc is None else acc + t
        for i in range(3):
            for core in range(2):
                at = a_cols + (2 * i + core) * few
                acc = acc + dot(held[:, at : at + few], ws[core][depth + i * few : depth + (i + 1) * few])
        total[...] = acc

        @pl.when(zh == zl)
        def _():
            own = pl.ds(pl.multiple_of(x * rows, rows), rows)
            cut = pl.ds(pl.multiple_of((step - 3 * side) * n, n), n)
            total[own] += e_ref[lax.rem(zl + side, 2), :, cut].astype(f32)

    @pl.when(step < 3)
    def _():
        multiply(weights[:2], 0)

    @pl.when(step >= 3)
    def _():
        multiply(weights[2:], 1)

    for j in range(4):
        for h in range(2):
            k = lax.rem(x + 4 - j, 4)
            at = pl.multiple_of(k * rows + lax.rem(zh + h, 2) * half, half)
            outs[2 * j + h][...] = total[pl.ds(at, half)].astype(bf16)


def output(info, e, units, ws):
    rows, half = units[0].shape[0], units[0].shape[0] // 2
    depth, width = ws[0][0].shape
    n = width // 3
    near = pl.BlockSpec((depth, n), lambda j: (0, jnp.minimum(j, 2)))
    far = pl.BlockSpec((depth, n), lambda j: (0, jnp.maximum(j - 3, 0)))
    return pl.pallas_call(
        output_kernel,
        grid=(6,),
        in_specs=[pl.BlockSpec(memory_space=pltpu.SMEM)]
        + [whole(v.shape) for v in [e] + units]
        + [near, near, far, far],
        out_specs=[pl.BlockSpec((half, n), lambda j: (0, j))] * 8,
        out_shape=[shape_of(half, 2 * width)] * 8,
        scratch_shapes=[
            pltpu.VMEM((4 * rows, units[0].shape[1]), bf16),
            pltpu.VMEM((4 * rows, n), f32),
        ],
        compiler_params=limit(24),
        cost_estimate=CHEAP,
        name="output",
    )(info, e, *units, *ws[0], *ws[1])


def finish_kernel(info_ref, *refs):
    parts, outs, held = refs[:8], refs[8:12], refs[12]
    total = parts[0][...].astype(f32)
    for ref in parts[1:]:
        total = total + ref[...].astype(f32)
    held[...] = total.astype(bf16)
    few = held.shape[0] // 4
    for k in range(4):
        outs[k][...] = held[pl.ds(pl.multiple_of(lax.rem(info_ref[2] + k, 4) * few, few), few)]


def finish(info, parts):
    half, cols = parts[0].shape
    return pl.pallas_call(
        finish_kernel,
        in_specs=[pl.BlockSpec(memory_space=pltpu.SMEM)] + [pl.BlockSpec(memory_space=pltpu.VMEM)] * 8,
        out_shape=[shape_of(half // 4, cols)] * 4,
        scratch_shapes=[pltpu.VMEM((half, cols), bf16)],
        compiler_params=limit(8),
        cost_estimate=CHEAP,
        name="finish",
    )(info, *parts)


def assemble_kernel(info_ref, *refs):
    out_ref = refs[4]
    zh, x = info_ref[0], info_ref[2]
    cols = refs[0].shape[1] // 2
    for i, k in enumerate((2, 1, 3, 0)):
        from_x = lax.rem(x + 4 - k, 4)
        for side in range(2):
            block = jnp.where(zh == side, 0, 4) + from_x
            out_ref[:, pl.ds(pl.multiple_of(block * cols, cols), cols)] = refs[i][:, side * cols : (side + 1) * cols]


def assemble(info, pieces):
    few, cols = pieces[0].shape
    return pl.pallas_call(
        assemble_kernel,
        in_specs=[pl.BlockSpec(memory_space=pltpu.SMEM)] + [pl.BlockSpec(memory_space=pltpu.VMEM)] * 4,
        out_shape=shape_of(few, 4 * cols),
        compiler_params=limit(4),
        cost_estimate=CHEAP,
        name="assemble",
    )(info, *pieces)


def shards(
    patches,
    patch_pos,
    tile_counts,
    pos_table,
    w_qkv,
    qk_gain,
    w_attn_out,
    w_mlp_in,
    mlp_bias,
    w_mlp_out,
    norm_gain,
):
    y, zh, c, zl, x = [lax.axis_index(a) for a in AXES]
    info = jnp.stack([zh, zl, x, x + 4, c])

    def count_to(d):
        image = d["zl"] * 4 + d["x"]
        if image % 2 != d["zl"]:
            d["zh"] += 1
        d["zl"], d["x"] = image % 2, image // 2 - d["y"] + 4
        return d

    wq = jnp.transpose(w_qkv, (1, 0, 2))
    wq_z = send(wq, zl=1)
    wq_c = send(wq, c=1)
    wm_c = send(w_mlp_in, c=1)

    cols = w_mlp_in.shape[0]
    pos = patch_pos[None]
    mine = jnp.stack([lax.dynamic_slice_in_dim(patches, (x + 4 * i) * cols, cols, 1) for i in range(2)])
    mine = cross(mine)
    pos_far = cross(pos)
    stat = measure(patches, pos, pos_table, 8)
    stat = after(stat, wq_c, wm_c)
    counts = route(after(tile_counts, stat), count_to)
    bias = mlp_bias[None]
    bias_far = send(after(bias, stat), c=1)
    e, normed = embed(info, mine, pos_far, cross(stat), pos_table, norm_gain[None])
    xs = {0: normed}
    for k in (2, 1, 3):
        xs[k] = send(normed, y=k)
    xs = [xs[k] for k in range(4)]

    wm_z = send(after(w_mlp_in, wq_z, normed, counts, bias_far), zl=1)
    wq_cz = send(after(wq_z, normed, counts, bias_far), c=1)
    wo = jnp.concatenate([after(w_attn_out, normed), w_mlp_out])

    def exchange(p):
        got = {k: send(p[k] if isinstance(p, (list, tuple)) else p, x=k) for k in (2, 1, 3)}
        return [p[0] if isinstance(p, (list, tuple)) else p] + [got[k] for k in (1, 2, 3)]

    first = project(info, xs, [wq, wq_z, wq_c, wq_cz])
    qkv = exchange(first)
    second = project(info, xs, [w_mlp_in, wm_z, wm_c, send(after(wm_z, first[0]), c=1)])
    pre = exchange(second)
    wo_z = send(after(wo, wm_z, first[0]), zl=1)
    q, kv = head_values([after(qkv[0], second[0])] + qkv[1:], qk_gain)
    kv_far = send(kv, c=1)
    attended = attend(info, counts, q, kv, kv_far)
    units = hidden_units(attended, pre, bias, bias_far)
    wo_c = send(after(wo, units), c=1)
    wo_cz = send(after(wo_z, units), c=1)
    units = exchange(units)

    parts = output(info, e, units, [[wo, wo_c], [wo_z, wo_cz]])
    moves = [(2, 1), (2, 0), (1, 1), (3, 1), (0, 1), (1, 0), (3, 0)]
    moved = {(j, h): send(parts[2 * j + h], y=j, zh=h) for j, h in moves}
    pieces = finish(info, [parts[0]] + [moved[m] for m in moves])
    return assemble(info, [cross(pieces[k], k) for k in (2, 1, 3, 0)])


def solution(mesh):
    fine = Mesh(mesh.devices.reshape([SIZES[a] for a in AXES]), AXES)
    dp, mp = ("y", "zh", "c"), ("zl", "x")
    placed = (
        P(dp, None),
        P(dp),
        P(mp),
        P(),
        P(mp, None, dp),
        P(),
        P(dp, mp),
        P(mp, dp),
        P(dp),
        P(dp, mp),
        P(),
    )
    return jax.shard_map(shards, mesh=fine, in_specs=placed, out_specs=P(dp + mp, None), check_vma=False)
```

```python
import functools
import itertools

import jax
import jax.numpy as jnp
from jax import lax
from jax.experimental import pallas as pl
from jax.experimental.pallas import tpu as pltpu
from jax.sharding import Mesh, PartitionSpec as P

TILE = 64
HS = 128
AXES = ("y", "zh", "c", "zl", "x")
SIZES = {"y": 4, "zh": 2, "c": 2, "zl": 2, "x": 4}
bf16 = jnp.bfloat16
f32 = jnp.float32
norm_eps = 1e-06
GROUPS = ((0, 1, 3), (2,))


def limit(mib):
    return pltpu.CompilerParams(vmem_limit_bytes=mib * 2**20)


CHEAP = pl.CostEstimate(flops=1000, bytes_accessed=1000, transcendentals=0)


def pairs(place):
    out = []
    for spot in itertools.product(*[range(SIZES[a]) for a in AXES]):
        here = dict(zip(AXES, spot))
        there = place(dict(here))
        ends = []
        for point in (here, there):
            index = 0
            for a in AXES:
                index = index * SIZES[a] + point[a] % SIZES[a]
            ends.append(index)
        out.append(tuple(ends))
    return out


def route(value, place):
    return lax.ppermute(value, AXES, pairs(place))


def send(value, **shift):
    def place(d):
        for a, by in shift.items():
            d[a] += by
        return d

    return route(value, place)


def cross(value, by=0):
    def place(d):
        d["zh"], d["zl"] = d["zl"], d["zh"]
        d["x"] += by
        return d

    return route(value, place)


def after(value, *others):
    return lax.optimization_barrier((value, *others))[0]


def dot(a, b):
    return jnp.dot(a, b, preferred_element_type=f32)


def whole(shape):
    return pl.BlockSpec(shape, lambda *_: (0,) * len(shape))


def shape_of(*shape, dtype=bf16):
    return jax.ShapeDtypeStruct(shape, dtype)


def lookup(chosen, refs):
    few = refs[0].shape[0]
    parts = [dot(chosen[:, i * few : (i + 1) * few], ref[...]) for i, ref in enumerate(refs)]
    return parts[0] + parts[1] + parts[2] + parts[3]


def choose(pos, chosen):
    rows, slots = chosen.shape
    at = jnp.broadcast_to(pos.astype(f32), (rows, rows)).T[:, 0:1]
    spots = lax.broadcasted_iota(jnp.int32, (rows, slots), 1)
    chosen[...] = (spots == at.astype(jnp.int32)).astype(f32).astype(bf16)


def measure_kernel(patches_ref, pos_ref, t0, t1, t2, t3, out_ref, chosen, means, devs):
    j, blocks = pl.program_id(0), pl.num_programs(0)
    rows, cols = patches_ref.shape

    @pl.when(j == 0)
    def _():
        choose(pos_ref[...], chosen)
        means[...] = jnp.zeros_like(means)
        devs[...] = jnp.zeros_like(devs)

    e = (patches_ref[...].astype(f32) + lookup(chosen, (t0, t1, t2, t3))).astype(bf16).astype(f32)
    mean = jnp.mean(e, axis=1, keepdims=True)
    dev = jnp.sum((e - mean) ** 2, axis=1, keepdims=True)
    lane = lax.broadcasted_iota(jnp.int32, (rows, 128), 1)
    means[...] = jnp.where(lane == j, mean, means[...])
    devs[...] = jnp.where(lane == j, dev, devs[...])

    @pl.when(j == blocks - 1)
    def _():
        count = blocks
        mu = jnp.sum(means[...], axis=1, keepdims=True) / count
        apart = jnp.where(lane < blocks, (means[...] - mu) ** 2, 0.0)
        total = jnp.sum(devs[...], axis=1, keepdims=True) + cols * jnp.sum(apart, axis=1, keepdims=True)
        scale = lax.rsqrt(total / (cols * count) + norm_eps)
        where = jnp.broadcast_to(pos_ref[...], out_ref.shape).astype(f32)
        row = lax.broadcasted_iota(jnp.int32, out_ref.shape, 0)
        out_ref[...] = jnp.where(row == 2, where, jnp.where(lane == 0, mu, scale).T[:8])


def measure(patches, pos, table, blocks):
    rows, cols, few = patches.shape[0], patches.shape[1] // blocks, table.shape[0] // 4
    return pl.pallas_call(
        measure_kernel,
        grid=(blocks,),
        in_specs=[pl.BlockSpec((rows, cols), lambda j: (0, j)), whole((1, rows))]
        + [pl.BlockSpec((few, cols), functools.partial(lambda i, j: (i, j), i)) for i in range(4)],
        out_specs=whole((8, rows)),
        out_shape=shape_of(8, rows, dtype=f32),
        scratch_shapes=[
            pltpu.VMEM((rows, table.shape[0]), bf16),
            pltpu.VMEM((rows, 128), f32),
            pltpu.VMEM((rows, 128), f32),
        ],
        compiler_params=limit(52),
        cost_estimate=CHEAP,
        name="measure",
    )(patches, pos, table, table, table, table)


def embed_kernel(info_ref, patches_ref, stat_ref, gain_ref, t0, t1, t2, t3, e_ref, normed_ref, chosen):
    @pl.when(pl.program_id(0) == 0)
    def _():
        choose(stat_ref[2:3], chosen)

    e = (patches_ref[0].astype(f32) + lookup(chosen, (t0, t1, t2, t3))).astype(bf16)
    e_ref[0] = e
    rows = e.shape[0]
    turned = jnp.concatenate([stat_ref[...]] * (rows // 8), axis=0).T
    normed_ref[0] = ((e.astype(f32) - turned[:, 0:1]) * turned[:, 1:2] * gain_ref[...]).astype(bf16)


def embed(info, patches, stat, table, gain):
    _, rows, cols = patches.shape
    few = table.shape[0] // 4
    return pl.pallas_call(
        embed_kernel,
        grid_spec=pltpu.PrefetchScalarGridSpec(
            num_scalar_prefetch=1,
            grid=(2,),
            in_specs=[
                pl.BlockSpec((1, rows, cols), lambda s, info: (s, 0, 0)),
                pl.BlockSpec((8, rows), lambda s, info: (0, 0)),
                pl.BlockSpec((1, cols), lambda s, info: (0, info[2 + s])),
            ]
            + [pl.BlockSpec((few, cols), functools.partial(lambda i, s, info: (i, info[2 + s]), i)) for i in range(4)],
            out_specs=[pl.BlockSpec((1, rows, cols), lambda s, info: (s, 0, 0))] * 2,
            scratch_shapes=[pltpu.VMEM((rows, table.shape[0]), bf16)],
        ),
        out_shape=[shape_of(2, rows, cols)] * 2,
        compiler_params=limit(52),
        cost_estimate=CHEAP,
        name="embed",
    )(info, patches, stat, gain, table, table, table, table)


def project_kernel(info_ref, x0, x1, x2, x3, w00, w01, w10, w11, o0, o1, o2, o3, held):
    rows = x0.shape[1]
    zl, x = info_ref[1], info_ref[2]

    @pl.when(pl.program_id(0) == 0)
    def _():
        for far, ref in enumerate((x0, x1, x2, x3)):
            k = lax.rem(8 - x - far, 4)
            for s in range(2):
                held[s, pl.ds(pl.multiple_of(k * rows, rows), rows)] = ref[lax.rem(zl + s, 2)]

    def weight(ref):
        w = ref[...]
        return w.reshape(w.shape[-2:])

    for core, (near, far) in enumerate(((w00, w01), (w10, w11))):
        got = dot(held[0], weight(near)) + dot(held[1], weight(far))
        n = got.shape[1]
        for k, ref in enumerate((o0, o1, o2, o3)):
            ref[:, core * n : (core + 1) * n] = got[k * rows : (k + 1) * rows].astype(ref.dtype)


def project(info, xs, ws):
    _, rows, depth = xs[0].shape
    if ws[0].ndim == 3:
        spec = pl.BlockSpec((1, depth, ws[0].shape[2]), lambda i: (i, 0, 0))
        steps, n = ws[0].shape[0], 2 * ws[0].shape[2]
    else:
        n = 512
        spec = pl.BlockSpec((depth, n // 2), lambda i: (0, i))
        steps = 2 * ws[0].shape[1] // n
    return pl.pallas_call(
        project_kernel,
        grid=(steps,),
        in_specs=[pl.BlockSpec(memory_space=pltpu.SMEM)] + [whole((2, rows, depth))] * 4 + [spec] * 4,
        out_specs=[pl.BlockSpec((rows, n), lambda i: (0, i))] * 4,
        out_shape=[shape_of(rows, steps * n, dtype=f32 if k == 0 else bf16) for k in range(4)],
        scratch_shapes=[pltpu.VMEM((2, 4 * rows, depth), bf16)],
        compiler_params=limit(20),
        cost_estimate=CHEAP,
        name="project",
    )(info, *xs, *ws)


def heads_kernel(p0, p1, p2, p3, gain_ref, q_ref, kv_ref):
    part = pl.program_id(0)
    gain = gain_ref[pl.ds(jnp.minimum(part, 1), 1)]
    for h in range(q_ref.shape[1] // HS):
        at = slice(h * HS, (h + 1) * HS)
        v = p0[:, at] + p1[:, at].astype(f32) + p2[:, at].astype(f32) + p3[:, at].astype(f32)
        centered = v - jnp.mean(v, axis=1, keepdims=True)
        spread = lax.rsqrt(jnp.mean(centered * centered, axis=1, keepdims=True) + norm_eps)
        normed = (centered * spread * gain).astype(bf16)

        @pl.when(part == 0)
        def _():
            q_ref[:, at] = normed

        @pl.when(part > 0)
        def _():
            kv_ref[0, :, at] = jnp.where(part == 1, normed.astype(f32), v).astype(bf16)


def head_values(parts, gain):
    rows, n = parts[0].shape[0], parts[0].shape[1] // 3
    return pl.pallas_call(
        heads_kernel,
        grid=(3,),
        in_specs=[pl.BlockSpec((rows, n), lambda i: (0, i))] * 4 + [whole(gain.shape)],
        out_specs=[whole((rows, n)), pl.BlockSpec((1, rows, n), lambda i: (jnp.maximum(i - 1, 0), 0, 0))],
        out_shape=[shape_of(rows, n), shape_of(2, rows, n)],
        compiler_params=limit(8),
        cost_estimate=CHEAP,
        name="heads",
    )(*parts, gain)


def hidden_kernel(att_ref, p0, p1, p2, p3, b0, b1, out_ref):
    step = pl.program_id(0)

    @pl.when(step == 0)
    def _():
        out_ref[...] = att_ref[...]

    @pl.when(step > 0)
    def _():
        bias = jnp.concatenate([b0[...], b1[...]], axis=1)
        v = p0[...] + p1[...].astype(f32) + p2[...].astype(f32) + p3[...].astype(f32) + bias
        out_ref[...] = (v * 0.5 * (1.0 + lax.erf(v * 0.5**0.5))).astype(bf16)


def hidden_units(attended, parts, bias, bias_far):
    rows, n = attended.shape
    steps = parts[0].shape[1] // n

    def block(i):
        return 0, jnp.maximum(i - 1, 0)

    return pl.pallas_call(
        hidden_kernel,
        grid=(1 + steps,),
        in_specs=[whole((rows, n))] + [pl.BlockSpec((rows, n), block)] * 4 + [pl.BlockSpec((1, n // 2), block)] * 2,
        out_specs=pl.BlockSpec((rows, n), lambda i: (0, i)),
        out_shape=shape_of(rows, (1 + steps) * n),
        compiler_params=limit(8),
        cost_estimate=CHEAP,
        name="hidden",
    )(attended, *parts, bias, bias_far)


def attend_kernel(info_ref, count_ref, q_ref, near_ref, far_ref, out_ref):
    core, live = info_ref[4], count_ref[0] * TILE
    rows, n = q_ref.shape
    slot = lax.broadcasted_iota(jnp.int32, (rows, rows), 1)
    heads = n // HS
    for h in range(heads):
        at = slice(h * HS, (h + 1) * HS)
        o = (h + heads // 2) % heads
        other = slice(o * HS, (o + 1) * HS)
        q = q_ref[:, at]
        score = []
        for k, first in ((near_ref[0, :, at], core * rows), (far_ref[0, :, other], (1 - core) * rows)):
            s = lax.dot_general(q, k, (((1,), (1,)), ((), ())), preferred_element_type=f32) * HS ** (-0.5)
            score.append(jnp.where(slot + first < live, s, -1e30))
        top = jnp.maximum(jnp.max(score[0], axis=1, keepdims=True), jnp.max(score[1], axis=1, keepdims=True))
        lifted = [jnp.exp(s - top) for s in score]
        total = jnp.sum(lifted[0], axis=1, keepdims=True) + jnp.sum(lifted[1], axis=1, keepdims=True)
        probs = [(v / total).astype(bf16) for v in lifted]
        out_ref[:, at] = (dot(probs[0], near_ref[1, :, at]) + dot(probs[1], far_ref[1, :, other])).astype(bf16)


def attend(info, count, q, near, far):
    return pl.pallas_call(
        attend_kernel,
        in_specs=[pl.BlockSpec(memory_space=pltpu.SMEM)] * 2 + [pl.BlockSpec(memory_space=pltpu.VMEM)] * 3,
        out_shape=shape_of(*q.shape),
        compiler_params=limit(6),
        cost_estimate=CHEAP,
        name="attend",
    )(info, count, q, near, far)


def output_kernel(ks, info_ref, e_ref, *refs):
    u_refs, weights, outs = refs[: len(ks)], refs[len(ks) : len(ks) + 4], refs[len(ks) + 4 : -2]
    held, total = refs[-2:]
    step = pl.program_id(0)
    rows, a_cols = u_refs[0].shape[0], u_refs[0].shape[1] // 4
    half, n = rows // 2, total.shape[1]
    zh, zl, x = info_ref[0], info_ref[1], info_ref[2]

    @pl.when(step == 0)
    def _():
        for i, ref in enumerate(u_refs):
            held[i * rows : (i + 1) * rows] = ref[...]

    def multiply(ws, side):
        depth = a_cols // 2
        few = (ws[0].shape[0] - depth) // 3
        acc = None
        for core in range(2):
            t = dot(held[:, core * depth : (core + 1) * depth], ws[core][:depth])
            acc = t if acc is None else acc + t
        for i in range(3):
            for core in range(2):
                at = a_cols + (2 * i + core) * few
                acc = acc + dot(held[:, at : at + few], ws[core][depth + i * few : depth + (i + 1) * few])
        total[...] = acc

        for i, k in enumerate(ks):

            @pl.when(jnp.logical_and(zh == zl, x == k))
            def _():
                cut = pl.ds(pl.multiple_of((step - 3 * side) * n, n), n)
                total[i * rows : (i + 1) * rows] += e_ref[lax.rem(zl + side, 2), :, cut].astype(f32)

    @pl.when(step < 3)
    def _():
        multiply(weights[:2], 0)

    @pl.when(step >= 3)
    def _():
        multiply(weights[2:], 1)

    for i in range(len(ks)):
        for h in range(2):
            at = pl.multiple_of(i * rows + lax.rem(zh + h, 2) * half, half)
            outs[2 * i + h][...] = total[pl.ds(at, half)].astype(bf16)


def output(info, e, ks, units, ws):
    rows, half = units[0].shape[0], units[0].shape[0] // 2
    depth, width = ws[0][0].shape
    n = width // 3
    near = pl.BlockSpec((depth, n), lambda j: (0, jnp.minimum(j, 2)))
    far = pl.BlockSpec((depth, n), lambda j: (0, jnp.maximum(j - 3, 0)))
    return pl.pallas_call(
        functools.partial(output_kernel, ks),
        grid=(6,),
        in_specs=[pl.BlockSpec(memory_space=pltpu.SMEM)]
        + [whole(v.shape) for v in [e] + units]
        + [near, near, far, far],
        out_specs=[pl.BlockSpec((half, n), lambda j: (0, j))] * (2 * len(ks)),
        out_shape=[shape_of(half, 2 * width)] * (2 * len(ks)),
        scratch_shapes=[
            pltpu.VMEM((len(ks) * rows, units[0].shape[1]), bf16),
            pltpu.VMEM((len(ks) * rows, n), f32),
        ],
        compiler_params=limit(24),
        cost_estimate=CHEAP,
        name="output",
    )(info, e, *units, *ws[0], *ws[1])


def finish_kernel(info_ref, *refs):
    parts, outs, held = refs[:8], refs[8:12], refs[12]
    total = parts[0][...].astype(f32)
    for ref in parts[1:]:
        total = total + ref[...].astype(f32)
    held[...] = total.astype(bf16)
    few = held.shape[0] // 4
    for k in range(4):
        outs[k][...] = held[pl.ds(pl.multiple_of(lax.rem(info_ref[2] + k, 4) * few, few), few)]


def finish(info, parts):
    half, cols = parts[0].shape
    return pl.pallas_call(
        finish_kernel,
        in_specs=[pl.BlockSpec(memory_space=pltpu.SMEM)] + [pl.BlockSpec(memory_space=pltpu.VMEM)] * 8,
        out_shape=[shape_of(half // 4, cols)] * 4,
        scratch_shapes=[pltpu.VMEM((half, cols), bf16)],
        compiler_params=limit(8),
        cost_estimate=CHEAP,
        name="finish",
    )(info, *parts)


def assemble_kernel(info_ref, *refs):
    out_ref = refs[4]
    zh, x = info_ref[0], info_ref[2]
    cols = refs[0].shape[1] // 2
    for i, k in enumerate((2, 1, 3, 0)):
        from_x = lax.rem(x + 4 - k, 4)
        for side in range(2):
            block = jnp.where(zh == side, 0, 4) + from_x
            out_ref[:, pl.ds(pl.multiple_of(block * cols, cols), cols)] = refs[i][:, side * cols : (side + 1) * cols]


def assemble(info, pieces):
    few, cols = pieces[0].shape
    return pl.pallas_call(
        assemble_kernel,
        in_specs=[pl.BlockSpec(memory_space=pltpu.SMEM)] + [pl.BlockSpec(memory_space=pltpu.VMEM)] * 4,
        out_shape=shape_of(few, 4 * cols),
        compiler_params=limit(4),
        cost_estimate=CHEAP,
        name="assemble",
    )(info, *pieces)


def shards(
    patches,
    patch_pos,
    tile_counts,
    pos_table,
    w_qkv,
    qk_gain,
    w_attn_out,
    w_mlp_in,
    mlp_bias,
    w_mlp_out,
    norm_gain,
):
    y, zh, c, zl, x = [lax.axis_index(a) for a in AXES]
    info = jnp.stack([zh, zl, x, x + 4, c])

    def count_to(d):
        image = d["zl"] * 4 + d["x"]
        if image % 2 != d["zl"]:
            d["zh"] += 1
        d["zl"], d["x"] = image % 2, image // 2 - d["y"] + 4
        return d

    wq = jnp.transpose(w_qkv, (1, 0, 2))
    wq_z = send(wq, zl=1)
    wq_c = send(wq, c=1)
    wm_c = send(w_mlp_in, c=1)

    cols = w_mlp_in.shape[0]
    pos = patch_pos[None]
    mine = jnp.stack([lax.dynamic_slice_in_dim(patches, (x + 4 * i) * cols, cols, 1) for i in range(2)])
    counts = route(tile_counts, count_to)
    mine = cross(after(mine, counts))
    stat = measure(patches, pos, pos_table, 8)
    stat = after(stat, wq_c, wm_c)
    bias = mlp_bias[None]
    bias_far = send(after(bias, stat), c=1)
    e, normed = embed(info, mine, cross(stat), pos_table, norm_gain[None])
    xs = {0: normed}
    for k in (2, 1, 3):
        xs[k] = send(normed, y=k)
    xs = [xs[k] for k in range(4)]

    wm_z = send(after(w_mlp_in, wq_z, normed, bias_far), zl=1)
    wq_cz = send(after(wq_z, normed, bias_far), c=1)
    wo = jnp.concatenate([after(w_attn_out, normed), w_mlp_out])

    def exchange(p):
        got = {k: send(p[k] if isinstance(p, (list, tuple)) else p, x=k) for k in (2, 1, 3)}
        return [p[0] if isinstance(p, (list, tuple)) else p] + [got[k] for k in (1, 2, 3)]

    first = project(info, xs, [wq, wq_z, wq_c, wq_cz])
    qkv = exchange(first)
    second = project(info, xs, [w_mlp_in, wm_z, wm_c, send(after(wm_z, first[0]), c=1)])
    pre = exchange(second)
    wo_z = send(after(wo, wm_z, first[0]), zl=1)
    q, kv = head_values([after(qkv[0], second[0])] + qkv[1:], qk_gain)
    kv_far = send(kv, c=1)
    attended = attend(info, counts, q, kv, kv_far)
    units = hidden_units(attended, pre, bias, bias_far)
    wo_c = send(after(wo, units), c=1)
    wo_cz = send(after(wo_z, units), c=1)

    def to_owner(k, h):
        def place(d):
            d["y"] += d["x"] + 4 - k
            d["zh"] += h
            return d

        return place

    far = {0: units, 1: send(units, x=1), 3: send(units, x=3)}
    far[2] = send(after(units, far[1], far[3]), x=2)
    parts = []
    for ks in GROUPS:
        got = output(info, e, ks, [far[k] for k in ks], [[wo, wo_c], [wo_z, wo_cz]])
        parts += [route(got[2 * i + h], to_owner(k, h)) for i, k in enumerate(ks) for h in (1, 0)]
    pieces = finish(info, parts)
    return assemble(info, [cross(pieces[k], k) for k in (2, 1, 3, 0)])


def solution(mesh):
    fine = Mesh(mesh.devices.reshape([SIZES[a] for a in AXES]), AXES)
    dp, mp = ("y", "zh", "c"), ("zl", "x")
    placed = (
        P(dp, None),
        P(dp),
        P(mp),
        P(),
        P(mp, None, dp),
        P(),
        P(dp, mp),
        P(mp, dp),
        P(dp),
        P(dp, mp),
        P(),
    )
    return jax.shard_map(shards, mesh=fine, in_specs=placed, out_specs=P(dp + mp, None), check_vma=False)
```

```python
import functools
import itertools

import jax
import jax.numpy as jnp
from jax import lax
from jax.experimental import pallas as pl
from jax.experimental.pallas import tpu as pltpu
from jax.sharding import Mesh, PartitionSpec as P

TILE = 64
HS = 128
AXES = ("y", "zh", "c", "zl", "x")
SIZES = {"y": 4, "zh": 2, "c": 2, "zl": 2, "x": 4}
bf16 = jnp.bfloat16
f32 = jnp.float32
norm_eps = 1e-06
GROUPS = ((0, 1, 3), (2,))


def limit(mib):
    return pltpu.CompilerParams(vmem_limit_bytes=mib * 2**20)


CHEAP = pl.CostEstimate(flops=1000, bytes_accessed=1000, transcendentals=0)


def pairs(place):
    out = []
    for spot in itertools.product(*[range(SIZES[a]) for a in AXES]):
        here = dict(zip(AXES, spot))
        there = place(dict(here))
        ends = []
        for point in (here, there):
            index = 0
            for a in AXES:
                index = index * SIZES[a] + point[a] % SIZES[a]
            ends.append(index)
        out.append(tuple(ends))
    return out


def route(value, place):
    return lax.ppermute(value, AXES, pairs(place))


def send(value, **shift):
    def place(d):
        for a, by in shift.items():
            d[a] += by
        return d

    return route(value, place)


def cross(value, by=0):
    def place(d):
        d["zh"], d["zl"] = d["zl"], d["zh"]
        d["x"] += by
        return d

    return route(value, place)


def after(value, *others):
    return lax.optimization_barrier((value, *others))[0]


def dot(a, b):
    return jnp.dot(a, b, preferred_element_type=f32)


def whole(shape):
    return pl.BlockSpec(shape, lambda *_: (0,) * len(shape))


def shape_of(*shape, dtype=bf16):
    return jax.ShapeDtypeStruct(shape, dtype)


def lookup(chosen, refs):
    few = refs[0].shape[0]
    parts = [dot(chosen[:, i * few : (i + 1) * few], ref[...]) for i, ref in enumerate(refs)]
    return parts[0] + parts[1] + parts[2] + parts[3]


def choose(pos, chosen):
    rows, slots = chosen.shape
    at = jnp.broadcast_to(pos.astype(f32), (rows, rows)).T[:, 0:1]
    spots = lax.broadcasted_iota(jnp.int32, (rows, slots), 1)
    chosen[...] = (spots == at.astype(jnp.int32)).astype(f32).astype(bf16)


def measure_kernel(patches_ref, pos_ref, t0, t1, t2, t3, out_ref, chosen, means, devs):
    j, blocks = pl.program_id(0), pl.num_programs(0)
    rows, cols = patches_ref.shape

    @pl.when(j == 0)
    def _():
        choose(pos_ref[...], chosen)
        means[...] = jnp.zeros_like(means)
        devs[...] = jnp.zeros_like(devs)

    e = (patches_ref[...].astype(f32) + lookup(chosen, (t0, t1, t2, t3))).astype(bf16).astype(f32)
    mean = jnp.mean(e, axis=1, keepdims=True)
    dev = jnp.sum((e - mean) ** 2, axis=1, keepdims=True)
    lane = lax.broadcasted_iota(jnp.int32, (rows, 128), 1)
    means[...] = jnp.where(lane == j, mean, means[...])
    devs[...] = jnp.where(lane == j, dev, devs[...])

    @pl.when(j == blocks - 1)
    def _():
        count = blocks
        mu = jnp.sum(means[...], axis=1, keepdims=True) / count
        apart = jnp.where(lane < blocks, (means[...] - mu) ** 2, 0.0)
        total = jnp.sum(devs[...], axis=1, keepdims=True) + cols * jnp.sum(apart, axis=1, keepdims=True)
        scale = lax.rsqrt(total / (cols * count) + norm_eps)
        where = jnp.broadcast_to(pos_ref[...], out_ref.shape).astype(f32)
        row = lax.broadcasted_iota(jnp.int32, out_ref.shape, 0)
        out_ref[...] = jnp.where(row == 2, where, jnp.where(lane == 0, mu, scale).T[:8])


def measure(patches, pos, table, blocks):
    rows, cols, few = patches.shape[0], patches.shape[1] // blocks, table.shape[0] // 4
    return pl.pallas_call(
        measure_kernel,
        grid=(blocks,),
        in_specs=[pl.BlockSpec((rows, cols), lambda j: (0, j)), whole((1, rows))]
        + [pl.BlockSpec((few, cols), functools.partial(lambda i, j: (i, j), i)) for i in range(4)],
        out_specs=whole((8, rows)),
        out_shape=shape_of(8, rows, dtype=f32),
        scratch_shapes=[
            pltpu.VMEM((rows, table.shape[0]), bf16),
            pltpu.VMEM((rows, 128), f32),
            pltpu.VMEM((rows, 128), f32),
        ],
        compiler_params=limit(52),
        cost_estimate=CHEAP,
        name="measure",
    )(patches, pos, table, table, table, table)


def embed_kernel(info_ref, patches_ref, stat_ref, gain_ref, t0, t1, t2, t3, e_ref, normed_ref, chosen):
    @pl.when(pl.program_id(0) == 0)
    def _():
        choose(stat_ref[2:3], chosen)

    e = (patches_ref[0].astype(f32) + lookup(chosen, (t0, t1, t2, t3))).astype(bf16)
    e_ref[0] = e
    rows = e.shape[0]
    turned = jnp.concatenate([stat_ref[...]] * (rows // 8), axis=0).T
    normed_ref[0] = ((e.astype(f32) - turned[:, 0:1]) * turned[:, 1:2] * gain_ref[...]).astype(bf16)


def embed(info, patches, stat, table, gain):
    _, rows, cols = patches.shape
    few = table.shape[0] // 4
    return pl.pallas_call(
        embed_kernel,
        grid_spec=pltpu.PrefetchScalarGridSpec(
            num_scalar_prefetch=1,
            grid=(2,),
            in_specs=[
                pl.BlockSpec((1, rows, cols), lambda s, info: (s, 0, 0)),
                pl.BlockSpec((8, rows), lambda s, info: (0, 0)),
                pl.BlockSpec((1, cols), lambda s, info: (0, info[2 + s])),
            ]
            + [pl.BlockSpec((few, cols), functools.partial(lambda i, s, info: (i, info[2 + s]), i)) for i in range(4)],
            out_specs=[pl.BlockSpec((1, rows, cols), lambda s, info: (s, 0, 0))] * 2,
            scratch_shapes=[pltpu.VMEM((rows, table.shape[0]), bf16)],
        ),
        out_shape=[shape_of(2, rows, cols)] * 2,
        compiler_params=limit(52),
        cost_estimate=CHEAP,
        name="embed",
    )(info, patches, stat, gain, table, table, table, table)


def project_kernel(info_ref, x0, x1, x2, x3, w00, w01, w10, w11, o0, o1, o2, o3, held):
    rows = x0.shape[1]
    zl, x = info_ref[1], info_ref[2]

    @pl.when(pl.program_id(0) == 0)
    def _():
        for far, ref in enumerate((x0, x1, x2, x3)):
            k = lax.rem(8 - x - far, 4)
            for s in range(2):
                held[s, pl.ds(pl.multiple_of(k * rows, rows), rows)] = ref[lax.rem(zl + s, 2)]

    def weight(ref):
        w = ref[...]
        return w.reshape(w.shape[-2:])

    for core, (near, far) in enumerate(((w00, w01), (w10, w11))):
        got = dot(held[0], weight(near)) + dot(held[1], weight(far))
        n = got.shape[1]
        for k, ref in enumerate((o0, o1, o2, o3)):
            ref[:, core * n : (core + 1) * n] = got[k * rows : (k + 1) * rows].astype(ref.dtype)


def project(info, xs, ws):
    _, rows, depth = xs[0].shape
    if ws[0].ndim == 3:
        spec = pl.BlockSpec((1, depth, ws[0].shape[2]), lambda i: (i, 0, 0))
        steps, n = ws[0].shape[0], 2 * ws[0].shape[2]
    else:
        n = 512
        spec = pl.BlockSpec((depth, n // 2), lambda i: (0, i))
        steps = 2 * ws[0].shape[1] // n
    return pl.pallas_call(
        project_kernel,
        grid=(steps,),
        in_specs=[pl.BlockSpec(memory_space=pltpu.SMEM)] + [whole((2, rows, depth))] * 4 + [spec] * 4,
        out_specs=[pl.BlockSpec((rows, n), lambda i: (0, i))] * 4,
        out_shape=[shape_of(rows, steps * n, dtype=f32 if k == 0 else bf16) for k in range(4)],
        scratch_shapes=[pltpu.VMEM((2, 4 * rows, depth), bf16)],
        compiler_params=limit(20),
        cost_estimate=CHEAP,
        name="project",
    )(info, *xs, *ws)


def heads_kernel(p0, p1, p2, p3, gain_ref, q_ref, kv_ref):
    part = pl.program_id(0)
    gain = gain_ref[pl.ds(jnp.minimum(part, 1), 1)]
    for h in range(q_ref.shape[1] // HS):
        at = slice(h * HS, (h + 1) * HS)
        v = p0[:, at] + p1[:, at].astype(f32) + p2[:, at].astype(f32) + p3[:, at].astype(f32)
        centered = v - jnp.mean(v, axis=1, keepdims=True)
        spread = lax.rsqrt(jnp.mean(centered * centered, axis=1, keepdims=True) + norm_eps)
        normed = (centered * spread * gain).astype(bf16)

        @pl.when(part == 0)
        def _():
            q_ref[:, at] = normed

        @pl.when(part > 0)
        def _():
            kv_ref[0, :, at] = jnp.where(part == 1, normed.astype(f32), v).astype(bf16)


def head_values(parts, gain):
    rows, n = parts[0].shape[0], parts[0].shape[1] // 3
    return pl.pallas_call(
        heads_kernel,
        grid=(3,),
        in_specs=[pl.BlockSpec((rows, n), lambda i: (0, i))] * 4 + [whole(gain.shape)],
        out_specs=[whole((rows, n)), pl.BlockSpec((1, rows, n), lambda i: (jnp.maximum(i - 1, 0), 0, 0))],
        out_shape=[shape_of(rows, n), shape_of(2, rows, n)],
        compiler_params=limit(8),
        cost_estimate=CHEAP,
        name="heads",
    )(*parts, gain)


def hidden_kernel(att_ref, p0, p1, p2, p3, b0, b1, out_ref):
    step = pl.program_id(0)

    @pl.when(step == 0)
    def _():
        out_ref[...] = att_ref[...]

    @pl.when(step > 0)
    def _():
        bias = jnp.concatenate([b0[...], b1[...]], axis=1)
        v = p0[...] + p1[...].astype(f32) + p2[...].astype(f32) + p3[...].astype(f32) + bias
        out_ref[...] = (v * 0.5 * (1.0 + lax.erf(v * 0.5**0.5))).astype(bf16)


def hidden_units(attended, parts, bias, bias_far):
    rows, n = attended.shape
    steps = parts[0].shape[1] // n

    def block(i):
        return 0, jnp.maximum(i - 1, 0)

    return pl.pallas_call(
        hidden_kernel,
        grid=(1 + steps,),
        in_specs=[whole((rows, n))] + [pl.BlockSpec((rows, n), block)] * 4 + [pl.BlockSpec((1, n // 2), block)] * 2,
        out_specs=pl.BlockSpec((rows, n), lambda i: (0, i)),
        out_shape=shape_of(rows, (1 + steps) * n),
        compiler_params=limit(8),
        cost_estimate=CHEAP,
        name="hidden",
    )(attended, *parts, bias, bias_far)


def attend_kernel(info_ref, count_ref, q_ref, near_ref, far_ref, out_ref):
    core, live = info_ref[4], count_ref[0] * TILE
    rows, n = q_ref.shape
    slot = lax.broadcasted_iota(jnp.int32, (rows, rows), 1)
    heads = n // HS
    for h in range(heads):
        at = slice(h * HS, (h + 1) * HS)
        o = (h + heads // 2) % heads
        other = slice(o * HS, (o + 1) * HS)
        q = q_ref[:, at]
        score = []
        for k, first in ((near_ref[0, :, at], core * rows), (far_ref[0, :, other], (1 - core) * rows)):
            s = lax.dot_general(q, k, (((1,), (1,)), ((), ())), preferred_element_type=f32) * HS ** (-0.5)
            score.append(jnp.where(slot + first < live, s, -1e30))
        top = jnp.maximum(jnp.max(score[0], axis=1, keepdims=True), jnp.max(score[1], axis=1, keepdims=True))
        lifted = [jnp.exp(s - top) for s in score]
        total = jnp.sum(lifted[0], axis=1, keepdims=True) + jnp.sum(lifted[1], axis=1, keepdims=True)
        probs = [(v / total).astype(bf16) for v in lifted]
        out_ref[:, at] = (dot(probs[0], near_ref[1, :, at]) + dot(probs[1], far_ref[1, :, other])).astype(bf16)


def attend(info, count, q, near, far):
    return pl.pallas_call(
        attend_kernel,
        in_specs=[pl.BlockSpec(memory_space=pltpu.SMEM)] * 2 + [pl.BlockSpec(memory_space=pltpu.VMEM)] * 3,
        out_shape=shape_of(*q.shape),
        compiler_params=limit(6),
        cost_estimate=CHEAP,
        name="attend",
    )(info, count, q, near, far)


def output_kernel(ks, info_ref, e_ref, *refs):
    u_refs, weights, outs = refs[: len(ks)], refs[len(ks) : len(ks) + 4], refs[len(ks) + 4 : -2]
    held, total = refs[-2:]
    step = pl.program_id(0)
    rows, a_cols = u_refs[0].shape[0], u_refs[0].shape[1] // 4
    half, n = rows // 2, total.shape[1]
    zh, zl, x = info_ref[0], info_ref[1], info_ref[2]

    @pl.when(step == 0)
    def _():
        for i, ref in enumerate(u_refs):
            held[i * rows : (i + 1) * rows] = ref[...]

    def multiply(ws, side):
        depth = a_cols // 2
        few = (ws[0].shape[0] - depth) // 3
        acc = None
        for core in range(2):
            t = dot(held[:, core * depth : (core + 1) * depth], ws[core][:depth])
            acc = t if acc is None else acc + t
        for i in range(3):
            for core in range(2):
                at = a_cols + (2 * i + core) * few
                acc = acc + dot(held[:, at : at + few], ws[core][depth + i * few : depth + (i + 1) * few])
        total[...] = acc

        for i, k in enumerate(ks):

            @pl.when(jnp.logical_and(zh == zl, x == k))
            def _():
                cut = pl.ds(pl.multiple_of((step - 3 * side) * n, n), n)
                total[i * rows : (i + 1) * rows] += e_ref[lax.rem(zl + side, 2), :, cut].astype(f32)

    @pl.when(step < 3)
    def _():
        multiply(weights[:2], 0)

    @pl.when(step >= 3)
    def _():
        multiply(weights[2:], 1)

    for i in range(len(ks)):
        for h in range(2):
            at = pl.multiple_of(i * rows + lax.rem(zh + h, 2) * half, half)
            outs[2 * i + h][...] = total[pl.ds(at, half)].astype(bf16)


def output(info, e, ks, units, ws):
    rows, half = units[0].shape[0], units[0].shape[0] // 2
    depth, width = ws[0][0].shape
    n = width // 3
    near = pl.BlockSpec((depth, n), lambda j: (0, jnp.minimum(j, 2)))
    far = pl.BlockSpec((depth, n), lambda j: (0, jnp.maximum(j - 3, 0)))
    return pl.pallas_call(
        functools.partial(output_kernel, ks),
        grid=(6,),
        in_specs=[pl.BlockSpec(memory_space=pltpu.SMEM)]
        + [whole(v.shape) for v in [e] + units]
        + [near, near, far, far],
        out_specs=[pl.BlockSpec((half, n), lambda j: (0, j))] * (2 * len(ks)),
        out_shape=[shape_of(half, 2 * width)] * (2 * len(ks)),
        scratch_shapes=[
            pltpu.VMEM((len(ks) * rows, units[0].shape[1]), bf16),
            pltpu.VMEM((len(ks) * rows, n), f32),
        ],
        compiler_params=limit(24),
        cost_estimate=CHEAP,
        name="output",
    )(info, e, *units, *ws[0], *ws[1])


def finish_kernel(info_ref, *refs):
    parts, outs, held = refs[:8], refs[8:12], refs[12]
    total = parts[0][...].astype(f32)
    for ref in parts[1:]:
        total = total + ref[...].astype(f32)
    held[...] = total.astype(bf16)
    few = held.shape[0] // 4
    for k in range(4):
        outs[k][...] = held[pl.ds(pl.multiple_of(lax.rem(info_ref[2] + k, 4) * few, few), few)]


def finish(info, parts):
    half, cols = parts[0].shape
    return pl.pallas_call(
        finish_kernel,
        in_specs=[pl.BlockSpec(memory_space=pltpu.SMEM)] + [pl.BlockSpec(memory_space=pltpu.VMEM)] * 8,
        out_shape=[shape_of(half // 4, cols)] * 4,
        scratch_shapes=[pltpu.VMEM((half, cols), bf16)],
        compiler_params=limit(8),
        cost_estimate=CHEAP,
        name="finish",
    )(info, *parts)


def assemble_kernel(info_ref, *refs):
    out_ref = refs[4]
    zh, x = info_ref[0], info_ref[2]
    cols = refs[0].shape[1] // 2
    for i, k in enumerate((2, 1, 3, 0)):
        from_x = lax.rem(x + 4 - k, 4)
        for side in range(2):
            block = jnp.where(zh == side, 0, 4) + from_x
            out_ref[:, pl.ds(pl.multiple_of(block * cols, cols), cols)] = refs[i][:, side * cols : (side + 1) * cols]


def assemble(info, pieces):
    few, cols = pieces[0].shape
    return pl.pallas_call(
        assemble_kernel,
        in_specs=[pl.BlockSpec(memory_space=pltpu.SMEM)] + [pl.BlockSpec(memory_space=pltpu.VMEM)] * 4,
        out_shape=shape_of(few, 4 * cols),
        compiler_params=limit(4),
        cost_estimate=CHEAP,
        name="assemble",
    )(info, *pieces)


def shards(
    patches,
    patch_pos,
    tile_counts,
    pos_table,
    w_qkv,
    qk_gain,
    w_attn_out,
    w_mlp_in,
    mlp_bias,
    w_mlp_out,
    norm_gain,
):
    y, zh, c, zl, x = [lax.axis_index(a) for a in AXES]
    info = jnp.stack([zh, zl, x, x + 4, c])

    def count_to(d):
        image = d["zl"] * 4 + d["x"]
        if image % 2 != d["zl"]:
            d["zh"] += 1
        d["zl"], d["x"] = image % 2, image // 2 - d["y"] + 4
        return d

    wq = jnp.transpose(w_qkv, (1, 0, 2))
    wq_z = send(wq, zl=1)
    wq_c = send(wq, c=1)
    wm_c = send(w_mlp_in, c=1)

    cols = w_mlp_in.shape[0]
    pos = patch_pos[None]
    mine = jnp.stack([lax.dynamic_slice_in_dim(patches, (x + 4 * i) * cols, cols, 1) for i in range(2)])
    mine = cross(mine)
    stat = measure(patches, pos, pos_table, 8)
    stat = after(stat, wq_c, wm_c)
    counts = route(after(tile_counts, stat), count_to)
    bias = mlp_bias[None]
    bias_far = send(after(bias, stat), c=1)
    e, normed = embed(info, mine, after(cross(stat), counts), pos_table, norm_gain[None])
    xs = {0: normed}
    for k in (2, 1, 3):
        xs[k] = send(normed, y=k)
    xs = [xs[k] for k in range(4)]

    wm_z = send(after(w_mlp_in, wq_z, normed, bias_far), zl=1)
    wq_cz = send(after(wq_z, normed, bias_far), c=1)
    wo = jnp.concatenate([after(w_attn_out, normed), w_mlp_out])

    def exchange(p):
        got = {k: send(p[k] if isinstance(p, (list, tuple)) else p, x=k) for k in (2, 1, 3)}
        return [p[0] if isinstance(p, (list, tuple)) else p] + [got[k] for k in (1, 2, 3)]

    first = project(info, xs, [wq, wq_z, wq_c, wq_cz])
    qkv = exchange(first)
    second = project(info, xs, [w_mlp_in, wm_z, wm_c, send(after(wm_z, first[0]), c=1)])
    pre = exchange(second)
    wo_z = send(after(wo, wm_z, first[0]), zl=1)
    q, kv = head_values([after(qkv[0], second[0])] + qkv[1:], qk_gain)
    kv_far = send(kv, c=1)
    attended = attend(info, counts, q, kv, kv_far)
    units = hidden_units(attended, pre, bias, bias_far)
    wo_c = send(after(wo, units), c=1)
    wo_cz = send(after(wo_z, units), c=1)

    def to_owner(k, h):
        def place(d):
            d["y"] += d["x"] + 4 - k
            d["zh"] += h
            return d

        return place

    far = {0: units, 1: send(units, x=1), 3: send(units, x=3)}
    far[2] = send(after(units, far[1], far[3]), x=2)
    parts = []
    for ks in GROUPS:
        got = output(info, e, ks, [far[k] for k in ks], [[wo, wo_c], [wo_z, wo_cz]])
        parts += [route(got[2 * i + h], to_owner(k, h)) for i, k in enumerate(ks) for h in (1, 0)]
    pieces = finish(info, parts)
    return assemble(info, [cross(pieces[k], k) for k in (2, 1, 3, 0)])


def solution(mesh):
    fine = Mesh(mesh.devices.reshape([SIZES[a] for a in AXES]), AXES)
    dp, mp = ("y", "zh", "c"), ("zl", "x")
    placed = (
        P(dp, None),
        P(dp),
        P(mp),
        P(),
        P(mp, None, dp),
        P(),
        P(dp, mp),
        P(mp, dp),
        P(dp),
        P(dp, mp),
        P(),
    )
    return jax.shard_map(shards, mesh=fine, in_specs=placed, out_specs=P(dp + mp, None), check_vma=False)
```

```python
import functools
import itertools

import jax
import jax.numpy as jnp
from jax import lax
from jax.experimental import pallas as pl
from jax.experimental.pallas import tpu as pltpu
from jax.sharding import Mesh, PartitionSpec as P

TILE = 64
HS = 128
AXES = ("y", "zh", "c", "zl", "x")
SIZES = {"y": 4, "zh": 2, "c": 2, "zl": 2, "x": 4}
bf16 = jnp.bfloat16
f32 = jnp.float32
norm_eps = 1e-06
GROUPS = ((0, 1, 3), (2,))


def limit(mib):
    return pltpu.CompilerParams(vmem_limit_bytes=mib * 2**20)


CHEAP = pl.CostEstimate(flops=1000, bytes_accessed=1000, transcendentals=0)


def pairs(place):
    out = []
    for spot in itertools.product(*[range(SIZES[a]) for a in AXES]):
        here = dict(zip(AXES, spot))
        there = place(dict(here))
        ends = []
        for point in (here, there):
            index = 0
            for a in AXES:
                index = index * SIZES[a] + point[a] % SIZES[a]
            ends.append(index)
        out.append(tuple(ends))
    return out


def route(value, place):
    return lax.ppermute(value, AXES, pairs(place))


def send(value, **shift):
    def place(d):
        for a, by in shift.items():
            d[a] += by
        return d

    return route(value, place)


def cross(value, by=0):
    def place(d):
        d["zh"], d["zl"] = d["zl"], d["zh"]
        d["x"] += by
        return d

    return route(value, place)


def after(value, *others):
    return lax.optimization_barrier((value, *others))[0]


def dot(a, b):
    return jnp.dot(a, b, preferred_element_type=f32)


def whole(shape):
    return pl.BlockSpec(shape, lambda *_: (0,) * len(shape))


def shape_of(*shape, dtype=bf16):
    return jax.ShapeDtypeStruct(shape, dtype)


def lookup(chosen, refs):
    few = refs[0].shape[0]
    parts = [dot(chosen[:, i * few : (i + 1) * few], ref[...]) for i, ref in enumerate(refs)]
    return parts[0] + parts[1] + parts[2] + parts[3]


def choose(pos, chosen):
    rows, slots = chosen.shape
    at = jnp.broadcast_to(pos.astype(f32), (rows, rows)).T[:, 0:1]
    spots = lax.broadcasted_iota(jnp.int32, (rows, slots), 1)
    chosen[...] = (spots == at.astype(jnp.int32)).astype(f32).astype(bf16)


def measure_kernel(patches_ref, pos_ref, t0, t1, t2, t3, out_ref, chosen, means, devs):
    j, blocks = pl.program_id(0), pl.num_programs(0)
    rows, cols = patches_ref.shape

    @pl.when(j == 0)
    def _():
        choose(pos_ref[...], chosen)
        means[...] = jnp.zeros_like(means)
        devs[...] = jnp.zeros_like(devs)

    e = (patches_ref[...].astype(f32) + lookup(chosen, (t0, t1, t2, t3))).astype(bf16).astype(f32)
    mean = jnp.mean(e, axis=1, keepdims=True)
    dev = jnp.sum((e - mean) ** 2, axis=1, keepdims=True)
    lane = lax.broadcasted_iota(jnp.int32, (rows, 128), 1)
    means[...] = jnp.where(lane == j, mean, means[...])
    devs[...] = jnp.where(lane == j, dev, devs[...])

    @pl.when(j == blocks - 1)
    def _():
        count = blocks
        mu = jnp.sum(means[...], axis=1, keepdims=True) / count
        apart = jnp.where(lane < blocks, (means[...] - mu) ** 2, 0.0)
        total = jnp.sum(devs[...], axis=1, keepdims=True) + cols * jnp.sum(apart, axis=1, keepdims=True)
        scale = lax.rsqrt(total / (cols * count) + norm_eps)
        where = jnp.broadcast_to(pos_ref[...], out_ref.shape).astype(f32)
        row = lax.broadcasted_iota(jnp.int32, out_ref.shape, 0)
        out_ref[...] = jnp.where(row == 2, where, jnp.where(lane == 0, mu, scale).T[:8])


def measure(patches, pos, table, blocks):
    rows, cols, few = patches.shape[0], patches.shape[1] // blocks, table.shape[0] // 4
    return pl.pallas_call(
        measure_kernel,
        grid=(blocks,),
        in_specs=[pl.BlockSpec((rows, cols), lambda j: (0, j)), whole((1, rows))]
        + [pl.BlockSpec((few, cols), functools.partial(lambda i, j: (i, j), i)) for i in range(4)],
        out_specs=whole((8, rows)),
        out_shape=shape_of(8, rows, dtype=f32),
        scratch_shapes=[
            pltpu.VMEM((rows, table.shape[0]), bf16),
            pltpu.VMEM((rows, 128), f32),
            pltpu.VMEM((rows, 128), f32),
        ],
        compiler_params=limit(52),
        cost_estimate=CHEAP,
        name="measure",
    )(patches, pos, table, table, table, table)


def embed_kernel(info_ref, patches_ref, stat_ref, gain_ref, t0, t1, t2, t3, e_ref, normed_ref, chosen):
    @pl.when(pl.program_id(0) == 0)
    def _():
        choose(stat_ref[2:3], chosen)

    e = (patches_ref[0].astype(f32) + lookup(chosen, (t0, t1, t2, t3))).astype(bf16)
    e_ref[0] = e
    rows = e.shape[0]
    turned = jnp.concatenate([stat_ref[...]] * (rows // 8), axis=0).T
    normed_ref[0] = ((e.astype(f32) - turned[:, 0:1]) * turned[:, 1:2] * gain_ref[...]).astype(bf16)


def embed(info, patches, stat, table, gain):
    _, rows, cols = patches.shape
    few = table.shape[0] // 4
    return pl.pallas_call(
        embed_kernel,
        grid_spec=pltpu.PrefetchScalarGridSpec(
            num_scalar_prefetch=1,
            grid=(2,),
            in_specs=[
                pl.BlockSpec((1, rows, cols), lambda s, info: (s, 0, 0)),
                pl.BlockSpec((8, rows), lambda s, info: (0, 0)),
                pl.BlockSpec((1, cols), lambda s, info: (0, info[2 + s])),
            ]
            + [pl.BlockSpec((few, cols), functools.partial(lambda i, s, info: (i, info[2 + s]), i)) for i in range(4)],
            out_specs=[pl.BlockSpec((1, rows, cols), lambda s, info: (s, 0, 0))] * 2,
            scratch_shapes=[pltpu.VMEM((rows, table.shape[0]), bf16)],
        ),
        out_shape=[shape_of(2, rows, cols)] * 2,
        compiler_params=limit(52),
        cost_estimate=CHEAP,
        name="embed",
    )(info, patches, stat, gain, table, table, table, table)


def project_kernel(info_ref, x0, x1, x2a, x2b, x3, w00, w01, w10, w11, o0, o1, o2, o3, held):
    rows = x0.shape[1]
    zl, x = info_ref[1], info_ref[2]

    @pl.when(pl.program_id(0) == 0)
    def _():
        for far, ref in enumerate((x0, x1, None, x3)):
            k = lax.rem(8 - x - far, 4)
            for s in range(2):
                side = lax.rem(zl + s, 2)
                block = jnp.where(side == 0, x2a[0], x2b[0]) if ref is None else ref[side]
                held[s, pl.ds(pl.multiple_of(k * rows, rows), rows)] = block

    def weight(ref):
        w = ref[...]
        return w.reshape(w.shape[-2:])

    for core, (near, far) in enumerate(((w00, w01), (w10, w11))):
        got = dot(held[0], weight(near)) + dot(held[1], weight(far))
        n = got.shape[1]
        for k, ref in enumerate((o0, o1, o2, o3)):
            ref[:, core * n : (core + 1) * n] = got[k * rows : (k + 1) * rows].astype(ref.dtype)


def project(info, xs, ws):
    _, rows, depth = xs[0].shape
    if ws[0].ndim == 3:
        spec = pl.BlockSpec((1, depth, ws[0].shape[2]), lambda i: (i, 0, 0))
        steps, n = ws[0].shape[0], 2 * ws[0].shape[2]
    else:
        n = 512
        spec = pl.BlockSpec((depth, n // 2), lambda i: (0, i))
        steps = 2 * ws[0].shape[1] // n
    return pl.pallas_call(
        project_kernel,
        grid=(steps,),
        in_specs=[pl.BlockSpec(memory_space=pltpu.SMEM)] + [whole(v.shape) for v in xs] + [spec] * 4,
        out_specs=[pl.BlockSpec((rows, n), lambda i: (0, i))] * 4,
        out_shape=[shape_of(rows, steps * n, dtype=f32 if k == 0 else bf16) for k in range(4)],
        scratch_shapes=[pltpu.VMEM((2, 4 * rows, depth), bf16)],
        compiler_params=limit(20),
        cost_estimate=CHEAP,
        name="project",
    )(info, *xs, *ws)


def heads_kernel(p0, p1, p2, p3, gain_ref, q_ref, kv_ref):
    part = pl.program_id(0)
    gain = gain_ref[pl.ds(jnp.minimum(part, 1), 1)]
    for h in range(q_ref.shape[1] // HS):
        at = slice(h * HS, (h + 1) * HS)
        v = p0[:, at] + p1[:, at].astype(f32) + p2[:, at].astype(f32) + p3[:, at].astype(f32)
        centered = v - jnp.mean(v, axis=1, keepdims=True)
        spread = lax.rsqrt(jnp.mean(centered * centered, axis=1, keepdims=True) + norm_eps)
        normed = (centered * spread * gain).astype(bf16)

        @pl.when(part == 0)
        def _():
            q_ref[:, at] = normed

        @pl.when(part > 0)
        def _():
            kv_ref[0, :, at] = jnp.where(part == 1, normed.astype(f32), v).astype(bf16)


def head_values(parts, gain):
    rows, n = parts[0].shape[0], parts[0].shape[1] // 3
    return pl.pallas_call(
        heads_kernel,
        grid=(3,),
        in_specs=[pl.BlockSpec((rows, n), lambda i: (0, i))] * 4 + [whole(gain.shape)],
        out_specs=[whole((rows, n)), pl.BlockSpec((1, rows, n), lambda i: (jnp.maximum(i - 1, 0), 0, 0))],
        out_shape=[shape_of(rows, n), shape_of(2, rows, n)],
        compiler_params=limit(8),
        cost_estimate=CHEAP,
        name="heads",
    )(*parts, gain)


def hidden_kernel(att_ref, p0, p1, p2, p3, b0, b1, out_ref):
    step = pl.program_id(0)

    @pl.when(step == 0)
    def _():
        out_ref[...] = att_ref[...]

    @pl.when(step > 0)
    def _():
        bias = jnp.concatenate([b0[...], b1[...]], axis=1)
        v = p0[...] + p1[...].astype(f32) + p2[...].astype(f32) + p3[...].astype(f32) + bias
        out_ref[...] = (v * 0.5 * (1.0 + lax.erf(v * 0.5**0.5))).astype(bf16)


def hidden_units(attended, parts, bias, bias_far):
    rows, n = attended.shape
    steps = parts[0].shape[1] // n

    def block(i):
        return 0, jnp.maximum(i - 1, 0)

    return pl.pallas_call(
        hidden_kernel,
        grid=(1 + steps,),
        in_specs=[whole((rows, n))] + [pl.BlockSpec((rows, n), block)] * 4 + [pl.BlockSpec((1, n // 2), block)] * 2,
        out_specs=pl.BlockSpec((rows, n), lambda i: (0, i)),
        out_shape=shape_of(rows, (1 + steps) * n),
        compiler_params=limit(8),
        cost_estimate=CHEAP,
        name="hidden",
    )(attended, *parts, bias, bias_far)


def attend_kernel(info_ref, count_ref, q_ref, near_ref, far_ref, out_ref):
    core, live = info_ref[4], count_ref[0] * TILE
    rows, n = q_ref.shape
    slot = lax.broadcasted_iota(jnp.int32, (rows, rows), 1)
    heads = n // HS
    for h in range(heads):
        at = slice(h * HS, (h + 1) * HS)
        o = (h + heads // 2) % heads
        other = slice(o * HS, (o + 1) * HS)
        q = q_ref[:, at]
        score = []
        for k, first in ((near_ref[0, :, at], core * rows), (far_ref[0, :, other], (1 - core) * rows)):
            s = lax.dot_general(q, k, (((1,), (1,)), ((), ())), preferred_element_type=f32) * HS ** (-0.5)
            score.append(jnp.where(slot + first < live, s, -1e30))
        top = jnp.maximum(jnp.max(score[0], axis=1, keepdims=True), jnp.max(score[1], axis=1, keepdims=True))
        lifted = [jnp.exp(s - top) for s in score]
        total = jnp.sum(lifted[0], axis=1, keepdims=True) + jnp.sum(lifted[1], axis=1, keepdims=True)
        probs = [(v / total).astype(bf16) for v in lifted]
        out_ref[:, at] = (dot(probs[0], near_ref[1, :, at]) + dot(probs[1], far_ref[1, :, other])).astype(bf16)


def attend(info, count, q, near, far):
    return pl.pallas_call(
        attend_kernel,
        in_specs=[pl.BlockSpec(memory_space=pltpu.SMEM)] * 2 + [pl.BlockSpec(memory_space=pltpu.VMEM)] * 3,
        out_shape=shape_of(*q.shape),
        compiler_params=limit(6),
        cost_estimate=CHEAP,
        name="attend",
    )(info, count, q, near, far)


def output_kernel(ks, count, info_ref, e_ref, *refs):
    u_refs, weights, outs = refs[:count], refs[count : count + 4], refs[count + 4 : -2]
    held, total = refs[-2:]
    step = pl.program_id(0)
    rows, a_cols = e_ref.shape[1], u_refs[0].shape[1] // 4
    half, n = rows // 2, total.shape[1]
    zh, zl, x = info_ref[0], info_ref[1], info_ref[2]

    @pl.when(step == 0)
    def _():
        at = 0
        for ref in u_refs:
            held[at : at + ref.shape[0]] = ref[...]
            at += ref.shape[0]

    def multiply(ws, side):
        depth = a_cols // 2
        few = (ws[0].shape[0] - depth) // 3
        acc = None
        for core in range(2):
            t = dot(held[:, core * depth : (core + 1) * depth], ws[core][:depth])
            acc = t if acc is None else acc + t
        for i in range(3):
            for core in range(2):
                at = a_cols + (2 * i + core) * few
                acc = acc + dot(held[:, at : at + few], ws[core][depth + i * few : depth + (i + 1) * few])
        total[...] = acc

        for i, k in enumerate(ks):

            @pl.when(jnp.logical_and(zh == zl, x == k))
            def _():
                cut = pl.ds(pl.multiple_of((step - 3 * side) * n, n), n)
                total[i * rows : (i + 1) * rows] += e_ref[lax.rem(zl + side, 2), :, cut].astype(f32)

    @pl.when(step < 3)
    def _():
        multiply(weights[:2], 0)

    @pl.when(step >= 3)
    def _():
        multiply(weights[2:], 1)

    for i in range(len(ks)):
        for h in range(2):
            at = pl.multiple_of(i * rows + lax.rem(zh + h, 2) * half, half)
            outs[2 * i + h][...] = total[pl.ds(at, half)].astype(bf16)


def output(info, e, ks, units, ws):
    rows, half = e.shape[1], e.shape[1] // 2
    depth, width = ws[0][0].shape
    n = width // 3
    near = pl.BlockSpec((depth, n), lambda j: (0, jnp.minimum(j, 2)))
    far = pl.BlockSpec((depth, n), lambda j: (0, jnp.maximum(j - 3, 0)))
    return pl.pallas_call(
        functools.partial(output_kernel, ks, len(units)),
        grid=(6,),
        in_specs=[pl.BlockSpec(memory_space=pltpu.SMEM)]
        + [whole(v.shape) for v in [e] + units]
        + [near, near, far, far],
        out_specs=[pl.BlockSpec((half, n), lambda j: (0, j))] * (2 * len(ks)),
        out_shape=[shape_of(half, 2 * width)] * (2 * len(ks)),
        scratch_shapes=[
            pltpu.VMEM((len(ks) * rows, units[0].shape[1]), bf16),
            pltpu.VMEM((len(ks) * rows, n), f32),
        ],
        compiler_params=limit(24),
        cost_estimate=CHEAP,
        name="output",
    )(info, e, *units, *ws[0], *ws[1])


def finish_kernel(info_ref, *refs):
    parts, outs, held = refs[:8], refs[8:12], refs[12]
    total = parts[0][...].astype(f32)
    for ref in parts[1:]:
        total = total + ref[...].astype(f32)
    held[...] = total.astype(bf16)
    few = held.shape[0] // 4
    for k in range(4):
        outs[k][...] = held[pl.ds(pl.multiple_of(lax.rem(info_ref[2] + k, 4) * few, few), few)]


def finish(info, parts):
    half, cols = parts[0].shape
    return pl.pallas_call(
        finish_kernel,
        in_specs=[pl.BlockSpec(memory_space=pltpu.SMEM)] + [pl.BlockSpec(memory_space=pltpu.VMEM)] * 8,
        out_shape=[shape_of(half // 4, cols)] * 4,
        scratch_shapes=[pltpu.VMEM((half, cols), bf16)],
        compiler_params=limit(8),
        cost_estimate=CHEAP,
        name="finish",
    )(info, *parts)


def assemble_kernel(info_ref, *refs):
    out_ref = refs[4]
    zh, x = info_ref[0], info_ref[2]
    cols = refs[0].shape[1] // 2
    for i, k in enumerate((2, 1, 3, 0)):
        from_x = lax.rem(x + 4 - k, 4)
        for side in range(2):
            block = jnp.where(zh == side, 0, 4) + from_x
            out_ref[:, pl.ds(pl.multiple_of(block * cols, cols), cols)] = refs[i][:, side * cols : (side + 1) * cols]


def assemble(info, pieces):
    few, cols = pieces[0].shape
    return pl.pallas_call(
        assemble_kernel,
        in_specs=[pl.BlockSpec(memory_space=pltpu.SMEM)] + [pl.BlockSpec(memory_space=pltpu.VMEM)] * 4,
        out_shape=shape_of(few, 4 * cols),
        compiler_params=limit(4),
        cost_estimate=CHEAP,
        name="assemble",
    )(info, *pieces)


def shards(
    patches,
    patch_pos,
    tile_counts,
    pos_table,
    w_qkv,
    qk_gain,
    w_attn_out,
    w_mlp_in,
    mlp_bias,
    w_mlp_out,
    norm_gain,
):
    y, zh, c, zl, x = [lax.axis_index(a) for a in AXES]
    info = jnp.stack([zh, zl, x, x + 4, c])

    def count_to(d):
        image = d["zl"] * 4 + d["x"]
        if image % 2 != d["zl"]:
            d["zh"] += 1
        d["zl"], d["x"] = image % 2, image // 2 - d["y"] + 4
        return d

    wq = jnp.transpose(w_qkv, (1, 0, 2))
    wq_z = send(wq, zl=1)
    wq_c = send(wq, c=1)
    wm_c = send(w_mlp_in, c=1)

    cols = w_mlp_in.shape[0]
    pos = patch_pos[None]
    mine = jnp.stack([lax.dynamic_slice_in_dim(patches, (x + 4 * i) * cols, cols, 1) for i in range(2)])
    mine = cross(mine)
    stat = measure(patches, pos, pos_table, 8)
    stat = after(stat, wq_c, wm_c)
    counts = route(after(tile_counts, stat), count_to)
    bias = mlp_bias[None]
    bias_far = send(after(bias, stat), c=1)
    e, normed = embed(info, mine, after(cross(stat), counts), pos_table, norm_gain[None])
    xs = {0: normed}
    for k in (1, 3):
        xs[k] = send(normed, y=k)
    xs = [xs[0], xs[1], send(xs[1][0:1], y=1), send(xs[3][1:2], y=3), xs[3]]

    wm_z = send(after(w_mlp_in, wq_z, mine, bias_far), zl=1)
    wq_cz = send(after(wq_z, normed, bias_far), c=1)
    wo = jnp.concatenate([after(w_attn_out, normed), w_mlp_out])

    def exchange(p):
        got = {k: send(p[k] if isinstance(p, (list, tuple)) else p, x=k) for k in (2, 1, 3)}
        return [p[0] if isinstance(p, (list, tuple)) else p] + [got[k] for k in (1, 2, 3)]

    first = project(info, xs, [wq, wq_z, wq_c, wq_cz])
    qkv = exchange(first)
    second = project(info, xs, [w_mlp_in, wm_z, wm_c, send(after(wm_z, first[0]), c=1)])
    pre = exchange(second)
    wo_z = send(after(wo, wm_z, first[0]), zl=1)
    q, kv = head_values([after(qkv[0], second[0])] + qkv[1:], qk_gain)
    kv_far = send(kv, c=1)
    attended = attend(info, counts, q, kv, kv_far)
    units = hidden_units(attended, pre, bias, bias_far)
    wo_c = send(after(wo, units), c=1)
    wo_cz = send(after(wo_z, units), c=1)

    def to_owner(k, h):
        def place(d):
            d["y"] += d["x"] + 4 - k
            d["zh"] += h
            return d

        return place

    far = {0: [units], 1: [send(units, x=1)], 3: [send(units, x=3)]}
    far[2] = [send(after(units, far[1][0], far[3][0]), x=2)]
    parts = []
    for ks in GROUPS:
        got = output(info, e, ks, [v for k in ks for v in far[k]], [[wo, wo_c], [wo_z, wo_cz]])
        parts += [route(got[2 * i + h], to_owner(k, h)) for i, k in enumerate(ks) for h in (1, 0)]
    pieces = finish(info, parts)
    return assemble(info, [cross(pieces[k], k) for k in (2, 1, 3, 0)])


def solution(mesh):
    fine = Mesh(mesh.devices.reshape([SIZES[a] for a in AXES]), AXES)
    dp, mp = ("y", "zh", "c"), ("zl", "x")
    placed = (
        P(dp, None),
        P(dp),
        P(mp),
        P(),
        P(mp, None, dp),
        P(),
        P(dp, mp),
        P(mp, dp),
        P(dp),
        P(dp, mp),
        P(),
    )
    return jax.shard_map(shards, mesh=fine, in_specs=placed, out_specs=P(dp + mp, None), check_vma=False)
```

```python
import functools
import itertools

import jax
import jax.numpy as jnp
from jax import lax
from jax.experimental import pallas as pl
from jax.experimental.pallas import tpu as pltpu
from jax.sharding import Mesh, PartitionSpec as P

TILE = 64
HS = 128
AXES = ("y", "zh", "c", "zl", "x")
SIZES = {"y": 4, "zh": 2, "c": 2, "zl": 2, "x": 4}
bf16 = jnp.bfloat16
f32 = jnp.float32
norm_eps = 1e-06
GROUPS = ((0, 1, 3), (2,))


def limit(mib):
    return pltpu.CompilerParams(vmem_limit_bytes=mib * 2**20)


CHEAP = pl.CostEstimate(flops=1000, bytes_accessed=1000, transcendentals=0)


def pairs(place):
    out = []
    for spot in itertools.product(*[range(SIZES[a]) for a in AXES]):
        here = dict(zip(AXES, spot))
        there = place(dict(here))
        ends = []
        for point in (here, there):
            index = 0
            for a in AXES:
                index = index * SIZES[a] + point[a] % SIZES[a]
            ends.append(index)
        out.append(tuple(ends))
    return out


def route(value, place):
    return lax.ppermute(value, AXES, pairs(place))


def send(value, **shift):
    def place(d):
        for a, by in shift.items():
            d[a] += by
        return d

    return route(value, place)


def cross(value, by=0):
    def place(d):
        d["zh"], d["zl"] = d["zl"], d["zh"]
        d["x"] += by
        return d

    return route(value, place)


def after(value, *others):
    return lax.optimization_barrier((value, *others))[0]


def dot(a, b):
    return jnp.dot(a, b, preferred_element_type=f32)


def whole(shape):
    return pl.BlockSpec(shape, lambda *_: (0,) * len(shape))


def shape_of(*shape, dtype=bf16):
    return jax.ShapeDtypeStruct(shape, dtype)


def lookup(chosen, refs):
    few = refs[0].shape[0]
    parts = [dot(chosen[:, i * few : (i + 1) * few], ref[...]) for i, ref in enumerate(refs)]
    return parts[0] + parts[1] + parts[2] + parts[3]


def choose(pos, chosen):
    rows, slots = chosen.shape
    at = jnp.broadcast_to(pos.astype(f32), (rows, rows)).T[:, 0:1]
    spots = lax.broadcasted_iota(jnp.int32, (rows, slots), 1)
    chosen[...] = (spots == at.astype(jnp.int32)).astype(f32).astype(bf16)


def measure_kernel(patches_ref, pos_ref, t0, t1, t2, t3, out_ref, chosen, means, devs):
    j, blocks = pl.program_id(0), pl.num_programs(0)
    rows, cols = patches_ref.shape

    @pl.when(j == 0)
    def _():
        choose(pos_ref[...], chosen)
        means[...] = jnp.zeros_like(means)
        devs[...] = jnp.zeros_like(devs)

    e = (patches_ref[...].astype(f32) + lookup(chosen, (t0, t1, t2, t3))).astype(bf16).astype(f32)
    mean = jnp.mean(e, axis=1, keepdims=True)
    dev = jnp.sum((e - mean) ** 2, axis=1, keepdims=True)
    lane = lax.broadcasted_iota(jnp.int32, (rows, 128), 1)
    means[...] = jnp.where(lane == j, mean, means[...])
    devs[...] = jnp.where(lane == j, dev, devs[...])

    @pl.when(j == blocks - 1)
    def _():
        count = blocks
        mu = jnp.sum(means[...], axis=1, keepdims=True) / count
        apart = jnp.where(lane < blocks, (means[...] - mu) ** 2, 0.0)
        total = jnp.sum(devs[...], axis=1, keepdims=True) + cols * jnp.sum(apart, axis=1, keepdims=True)
        scale = lax.rsqrt(total / (cols * count) + norm_eps)
        where = jnp.broadcast_to(pos_ref[...], out_ref.shape).astype(f32)
        row = lax.broadcasted_iota(jnp.int32, out_ref.shape, 0)
        out_ref[...] = jnp.where(row == 2, where, jnp.where(lane == 0, mu, scale).T[:8])


def measure(patches, pos, table, blocks):
    rows, cols, few = patches.shape[0], patches.shape[1] // blocks, table.shape[0] // 4
    return pl.pallas_call(
        measure_kernel,
        grid=(blocks,),
        in_specs=[pl.BlockSpec((rows, cols), lambda j: (0, j)), whole((1, rows))]
        + [pl.BlockSpec((few, cols), functools.partial(lambda i, j: (i, j), i)) for i in range(4)],
        out_specs=whole((8, rows)),
        out_shape=shape_of(8, rows, dtype=f32),
        scratch_shapes=[
            pltpu.VMEM((rows, table.shape[0]), bf16),
            pltpu.VMEM((rows, 128), f32),
            pltpu.VMEM((rows, 128), f32),
        ],
        compiler_params=limit(52),
        cost_estimate=CHEAP,
        name="measure",
    )(patches, pos, table, table, table, table)


def embed_kernel(info_ref, patches_ref, stat_ref, gain_ref, t0, t1, t2, t3, e_ref, normed_ref, chosen):
    @pl.when(pl.program_id(0) == 0)
    def _():
        choose(stat_ref[2:3], chosen)

    e = (patches_ref[0].astype(f32) + lookup(chosen, (t0, t1, t2, t3))).astype(bf16)
    e_ref[0] = e
    rows = e.shape[0]
    turned = jnp.concatenate([stat_ref[...]] * (rows // 8), axis=0).T
    normed_ref[0] = ((e.astype(f32) - turned[:, 0:1]) * turned[:, 1:2] * gain_ref[...]).astype(bf16)


def embed(info, patches, stat, table, gain):
    _, rows, cols = patches.shape
    few = table.shape[0] // 4
    return pl.pallas_call(
        embed_kernel,
        grid_spec=pltpu.PrefetchScalarGridSpec(
            num_scalar_prefetch=1,
            grid=(2,),
            in_specs=[
                pl.BlockSpec((1, rows, cols), lambda s, info: (s, 0, 0)),
                pl.BlockSpec((8, rows), lambda s, info: (0, 0)),
                pl.BlockSpec((1, cols), lambda s, info: (0, info[2 + s])),
            ]
            + [pl.BlockSpec((few, cols), functools.partial(lambda i, s, info: (i, info[2 + s]), i)) for i in range(4)],
            out_specs=[pl.BlockSpec((1, rows, cols), lambda s, info: (s, 0, 0))] * 2,
            scratch_shapes=[pltpu.VMEM((rows, table.shape[0]), bf16)],
        ),
        out_shape=[shape_of(2, rows, cols)] * 2,
        compiler_params=limit(52),
        cost_estimate=CHEAP,
        name="embed",
    )(info, patches, stat, gain, table, table, table, table)


def project_kernel(info_ref, x0, x1, x2a, x2b, x3, w00, w01, w10, w11, o0, o1, o2, o3, held):
    rows = x0.shape[1]
    zl, x = info_ref[1], info_ref[2]

    @pl.when(pl.program_id(0) == 0)
    def _():
        for far, ref in enumerate((x0, x1, None, x3)):
            k = lax.rem(8 - x - far, 4)
            for s in range(2):
                side = lax.rem(zl + s, 2)
                block = jnp.where(side == 0, x2a[0], x2b[0]) if ref is None else ref[side]
                held[s, pl.ds(pl.multiple_of(k * rows, rows), rows)] = block

    def weight(ref):
        w = ref[...]
        return w.reshape(w.shape[-2:])

    for core, (near, far) in enumerate(((w00, w01), (w10, w11))):
        got = dot(held[0], weight(near)) + dot(held[1], weight(far))
        n = got.shape[1]
        for k, ref in enumerate((o0, o1, o2, o3)):
            ref[:, core * n : (core + 1) * n] = got[k * rows : (k + 1) * rows].astype(ref.dtype)


def project(info, xs, ws):
    _, rows, depth = xs[0].shape
    if ws[0].ndim == 3:
        spec = pl.BlockSpec((1, depth, ws[0].shape[2]), lambda i: (i, 0, 0))
        steps, n = ws[0].shape[0], 2 * ws[0].shape[2]
    else:
        n = 512
        spec = pl.BlockSpec((depth, n // 2), lambda i: (0, i))
        steps = 2 * ws[0].shape[1] // n
    return pl.pallas_call(
        project_kernel,
        grid=(steps,),
        in_specs=[pl.BlockSpec(memory_space=pltpu.SMEM)] + [whole(v.shape) for v in xs] + [spec] * 4,
        out_specs=[pl.BlockSpec((rows, n), lambda i: (0, i))] * 4,
        out_shape=[shape_of(rows, steps * n, dtype=f32 if k == 0 else bf16) for k in range(4)],
        scratch_shapes=[pltpu.VMEM((2, 4 * rows, depth), bf16)],
        compiler_params=limit(20),
        cost_estimate=CHEAP,
        name="project",
    )(info, *xs, *ws)


def heads_kernel(p0, p1, p2, p3, gain_ref, q_ref, kv_ref):
    part = pl.program_id(0)
    gain = gain_ref[pl.ds(jnp.minimum(part, 1), 1)]
    for h in range(q_ref.shape[1] // HS):
        at = slice(h * HS, (h + 1) * HS)
        v = p0[:, at] + p1[:, at].astype(f32) + p2[:, at].astype(f32) + p3[:, at].astype(f32)
        centered = v - jnp.mean(v, axis=1, keepdims=True)
        spread = lax.rsqrt(jnp.mean(centered * centered, axis=1, keepdims=True) + norm_eps)
        normed = (centered * spread * gain).astype(bf16)

        @pl.when(part == 0)
        def _():
            q_ref[:, at] = normed

        @pl.when(part > 0)
        def _():
            kv_ref[0, :, at] = jnp.where(part == 1, normed.astype(f32), v).astype(bf16)


def head_values(parts, gain):
    rows, n = parts[0].shape[0], parts[0].shape[1] // 3
    return pl.pallas_call(
        heads_kernel,
        grid=(3,),
        in_specs=[pl.BlockSpec((rows, n), lambda i: (0, i))] * 4 + [whole(gain.shape)],
        out_specs=[whole((rows, n)), pl.BlockSpec((1, rows, n), lambda i: (jnp.maximum(i - 1, 0), 0, 0))],
        out_shape=[shape_of(rows, n), shape_of(2, rows, n)],
        compiler_params=limit(8),
        cost_estimate=CHEAP,
        name="heads",
    )(*parts, gain)


def hidden_kernel(att_ref, p0, p1, p2, p3, b0, b1, out_ref):
    step = pl.program_id(0)

    @pl.when(step == 0)
    def _():
        out_ref[...] = att_ref[...]

    @pl.when(step > 0)
    def _():
        bias = jnp.concatenate([b0[...], b1[...]], axis=1)
        v = p0[...] + p1[...].astype(f32) + p2[...].astype(f32) + p3[...].astype(f32) + bias
        out_ref[...] = (v * 0.5 * (1.0 + lax.erf(v * 0.5**0.5))).astype(bf16)


def hidden_units(attended, parts, bias, bias_far):
    rows, n = attended.shape
    steps = parts[0].shape[1] // n

    def block(i):
        return 0, jnp.maximum(i - 1, 0)

    return pl.pallas_call(
        hidden_kernel,
        grid=(1 + steps,),
        in_specs=[whole((rows, n))] + [pl.BlockSpec((rows, n), block)] * 4 + [pl.BlockSpec((1, n // 2), block)] * 2,
        out_specs=pl.BlockSpec((rows, n), lambda i: (0, i)),
        out_shape=shape_of(rows, (1 + steps) * n),
        compiler_params=limit(8),
        cost_estimate=CHEAP,
        name="hidden",
    )(attended, *parts, bias, bias_far)


def attend_kernel(info_ref, count_ref, q_ref, near_ref, far_ref, out_ref):
    core, live = info_ref[4], count_ref[0] * TILE
    rows, n = q_ref.shape
    slot = lax.broadcasted_iota(jnp.int32, (rows, rows), 1)
    heads = n // HS
    for h in range(heads):
        at = slice(h * HS, (h + 1) * HS)
        o = (h + heads // 2) % heads
        other = slice(o * HS, (o + 1) * HS)
        q = q_ref[:, at]
        score = []
        for k, first in ((near_ref[0, :, at], core * rows), (far_ref[0, :, other], (1 - core) * rows)):
            s = lax.dot_general(q, k, (((1,), (1,)), ((), ())), preferred_element_type=f32) * HS ** (-0.5)
            score.append(jnp.where(slot + first < live, s, -1e30))
        top = jnp.maximum(jnp.max(score[0], axis=1, keepdims=True), jnp.max(score[1], axis=1, keepdims=True))
        lifted = [jnp.exp(s - top) for s in score]
        total = jnp.sum(lifted[0], axis=1, keepdims=True) + jnp.sum(lifted[1], axis=1, keepdims=True)
        probs = [(v / total).astype(bf16) for v in lifted]
        out_ref[:, at] = (dot(probs[0], near_ref[1, :, at]) + dot(probs[1], far_ref[1, :, other])).astype(bf16)


def attend(info, count, q, near, far):
    return pl.pallas_call(
        attend_kernel,
        in_specs=[pl.BlockSpec(memory_space=pltpu.SMEM)] * 2 + [pl.BlockSpec(memory_space=pltpu.VMEM)] * 3,
        out_shape=shape_of(*q.shape),
        compiler_params=limit(6),
        cost_estimate=CHEAP,
        name="attend",
    )(info, count, q, near, far)


def output_kernel(ks, count, info_ref, e_ref, *refs):
    u_refs, weights, outs = refs[:count], refs[count : count + 4], refs[count + 4 : -2]
    held, total = refs[-2:]
    step = pl.program_id(0)
    rows, a_cols = e_ref.shape[1], u_refs[0].shape[1] // 4
    half, n = rows // 2, total.shape[1]
    zh, zl, x = info_ref[0], info_ref[1], info_ref[2]

    @pl.when(step == 0)
    def _():
        at = 0
        for ref in u_refs:
            held[at : at + ref.shape[0]] = ref[...]
            at += ref.shape[0]

    def multiply(ws, side):
        depth = a_cols // 2
        few = (ws[0].shape[0] - depth) // 3
        acc = None
        for core in range(2):
            t = dot(held[:, core * depth : (core + 1) * depth], ws[core][:depth])
            acc = t if acc is None else acc + t
        for i in range(3):
            for core in range(2):
                at = a_cols + (2 * i + core) * few
                acc = acc + dot(held[:, at : at + few], ws[core][depth + i * few : depth + (i + 1) * few])
        total[...] = acc

        for i, k in enumerate(ks):

            @pl.when(jnp.logical_and(zh == zl, x == k))
            def _():
                cut = pl.ds(pl.multiple_of((step - 3 * side) * n, n), n)
                total[i * rows : (i + 1) * rows] += e_ref[lax.rem(zl + side, 2), :, cut].astype(f32)

    @pl.when(step < 3)
    def _():
        multiply(weights[:2], 0)

    @pl.when(step >= 3)
    def _():
        multiply(weights[2:], 1)

    for i in range(len(ks)):
        for h in range(2):
            at = pl.multiple_of(i * rows + lax.rem(zh + h, 2) * half, half)
            outs[2 * i + h][...] = total[pl.ds(at, half)].astype(bf16)


def output(info, e, ks, units, ws):
    rows, half = e.shape[1], e.shape[1] // 2
    depth, width = ws[0][0].shape
    n = width // 3
    near = pl.BlockSpec((depth, n), lambda j: (0, jnp.minimum(j, 2)))
    far = pl.BlockSpec((depth, n), lambda j: (0, jnp.maximum(j - 3, 0)))
    return pl.pallas_call(
        functools.partial(output_kernel, ks, len(units)),
        grid=(6,),
        in_specs=[pl.BlockSpec(memory_space=pltpu.SMEM)]
        + [whole(v.shape) for v in [e] + units]
        + [near, near, far, far],
        out_specs=[pl.BlockSpec((half, n), lambda j: (0, j))] * (2 * len(ks)),
        out_shape=[shape_of(half, 2 * width)] * (2 * len(ks)),
        scratch_shapes=[
            pltpu.VMEM((len(ks) * rows, units[0].shape[1]), bf16),
            pltpu.VMEM((len(ks) * rows, n), f32),
        ],
        compiler_params=limit(24),
        cost_estimate=CHEAP,
        name="output",
    )(info, e, *units, *ws[0], *ws[1])


def finish_kernel(info_ref, *refs):
    parts, outs, held = refs[:8], refs[8:12], refs[12]
    total = parts[0][...].astype(f32)
    for ref in parts[1:]:
        total = total + ref[...].astype(f32)
    held[...] = total.astype(bf16)
    few = held.shape[0] // 4
    for k in range(4):
        outs[k][...] = held[pl.ds(pl.multiple_of(lax.rem(info_ref[2] + k, 4) * few, few), few)]


def finish(info, parts):
    half, cols = parts[0].shape
    return pl.pallas_call(
        finish_kernel,
        in_specs=[pl.BlockSpec(memory_space=pltpu.SMEM)] + [pl.BlockSpec(memory_space=pltpu.VMEM)] * 8,
        out_shape=[shape_of(half // 4, cols)] * 4,
        scratch_shapes=[pltpu.VMEM((half, cols), bf16)],
        compiler_params=limit(8),
        cost_estimate=CHEAP,
        name="finish",
    )(info, *parts)


def assemble_kernel(info_ref, *refs):
    out_ref = refs[4]
    zh, x = info_ref[0], info_ref[2]
    cols = refs[0].shape[1] // 2
    for i, k in enumerate((2, 1, 3, 0)):
        from_x = lax.rem(x + 4 - k, 4)
        for side in range(2):
            block = jnp.where(zh == side, 0, 4) + from_x
            out_ref[:, pl.ds(pl.multiple_of(block * cols, cols), cols)] = refs[i][:, side * cols : (side + 1) * cols]


def assemble(info, pieces):
    few, cols = pieces[0].shape
    return pl.pallas_call(
        assemble_kernel,
        in_specs=[pl.BlockSpec(memory_space=pltpu.SMEM)] + [pl.BlockSpec(memory_space=pltpu.VMEM)] * 4,
        out_shape=shape_of(few, 4 * cols),
        compiler_params=limit(4),
        cost_estimate=CHEAP,
        name="assemble",
    )(info, *pieces)


def shards(
    patches,
    patch_pos,
    tile_counts,
    pos_table,
    w_qkv,
    qk_gain,
    w_attn_out,
    w_mlp_in,
    mlp_bias,
    w_mlp_out,
    norm_gain,
):
    y, zh, c, zl, x = [lax.axis_index(a) for a in AXES]
    info = jnp.stack([zh, zl, x, x + 4, c])

    def count_to(d):
        image = d["zl"] * 4 + d["x"]
        if image % 2 != d["zl"]:
            d["zh"] += 1
        d["zl"], d["x"] = image % 2, image // 2 - d["y"] + 4
        return d

    wq = jnp.transpose(w_qkv, (1, 0, 2))
    wq_z = send(wq, zl=1)
    wq_c = send(wq, c=1)
    wm_c = send(w_mlp_in, c=1)

    cols = w_mlp_in.shape[0]
    pos = patch_pos[None]
    mine = jnp.stack([lax.dynamic_slice_in_dim(patches, (x + 4 * i) * cols, cols, 1) for i in range(2)])
    mine = cross(mine)
    stat = measure(patches, pos, pos_table, 8)
    stat = after(stat, wq_c, wm_c)
    counts = route(after(tile_counts, stat), count_to)
    bias = mlp_bias[None]
    bias_far = send(after(bias, stat), c=1)
    e, normed = embed(info, mine, after(cross(stat), counts), pos_table, norm_gain[None])
    xs = {0: normed}
    for k in (1, 3):
        xs[k] = send(normed, y=k)
    xs = [xs[0], xs[1], send(xs[1][0:1], y=1), send(xs[3][1:2], y=3), xs[3]]

    wm_z = send(after(w_mlp_in, wq_z, normed, bias_far), zl=1)
    wq_cz = send(after(wq_z, normed, bias_far), c=1)
    wo = jnp.concatenate([after(w_attn_out, normed), w_mlp_out])

    def exchange(p):
        got = {k: send(p[k] if isinstance(p, (list, tuple)) else p, x=k) for k in (2, 1, 3)}
        return [p[0] if isinstance(p, (list, tuple)) else p] + [got[k] for k in (1, 2, 3)]

    first = project(info, xs, [wq, wq_z, wq_c, wq_cz])
    qkv = exchange(first)
    second = project(info, xs, [w_mlp_in, wm_z, wm_c, send(after(wm_z, first[0]), c=1)])
    pre = exchange(second)
    wo_z = send(after(wo, wm_z, first[0]), zl=1)
    q, kv = head_values([after(qkv[0], second[0])] + qkv[1:], qk_gain)
    kv_far = send(kv, c=1)
    attended = attend(info, counts, q, kv, kv_far)
    units = hidden_units(attended, pre, bias, bias_far)
    wo_c = send(after(wo, units), c=1)
    wo_cz = send(after(wo_z, units), c=1)

    def to_owner(k, h):
        def place(d):
            d["y"] += d["x"] + 4 - k
            d["zh"] += h
            return d

        return place

    far = {0: [units], 1: [send(units, x=1)], 3: [send(units, x=3)]}
    far[2] = [send(after(units, far[1][0], far[3][0]), x=2)]
    parts = []
    for ks in GROUPS:
        got = output(info, e, ks, [v for k in ks for v in far[k]], [[wo, wo_c], [wo_z, wo_cz]])
        parts += [route(got[2 * i + h], to_owner(k, h)) for i, k in enumerate(ks) for h in (1, 0)]
    pieces = finish(info, parts)
    return assemble(info, [cross(pieces[k], k) for k in (2, 1, 3, 0)])


def solution(mesh):
    fine = Mesh(mesh.devices.reshape([SIZES[a] for a in AXES]), AXES)
    dp, mp = ("y", "zh", "c"), ("zl", "x")
    placed = (
        P(dp, None),
        P(dp),
        P(mp),
        P(),
        P(mp, None, dp),
        P(),
        P(dp, mp),
        P(mp, dp),
        P(dp),
        P(dp, mp),
        P(),
    )
    return jax.shard_map(shards, mesh=fine, in_specs=placed, out_specs=P(dp + mp, None), check_vma=False)
```
